32 devices in a mesh: section: 2 (over y), len: 4 (over z), ht: 2 (over x), wd: 2 (over core).
Axes of the slice: x: 2, y: 2, z: 4, core: 2. Of those that a mesh axis runs over, the one named last changes fastest.
Arguments:
- positions: float32 [3, 64, 4, 4, 128], P(None, ('section', 'len'), 'ht', 'wd'), parts along dimension 1, may hold values from 0 to 1
- velocities: float32 [3, 64, 4, 4, 128], P(None, ('section', 'len'), 'ht', 'wd'), parts along dimension 1, may hold values from -3 to 3
- radius: float32 [64, 4, 4, 128], P(('section', 'len'), 'ht', 'wd'), parts along dimension 0, may hold values from 0.3 to 0.6
- counts: int32 [64, 4, 4], P(('section', 'len'), 'ht', 'wd'), parts along dimension 0, may hold values from 0 to 128, as said below
- cell_index: int32 [64, 4, 4, 128], P(('section', 'len'), 'ht', 'wd'), parts along dimension 0, may hold values from 0 to 1023
- fluid_velocity: float32 [3, 8192], P(None, ('section', 'len', 'ht', 'wd')), parts along dimension 1, may hold values from -6 to 6
- plan: int32 [8, 2, 2, 32, 1], P(('section', 'len'), 'ht', 'wd'), parts along dimension 0, may hold values from 0 to 3; in each aligned block of 32 rows (0 to 31, 32 to 63, ..., all dimensions but the last counted through in order) at most 16 rows name the same one
Outputs:
- moved: float32 [8, 2, 2, 512, 128], P(None, 'ht', 'wd', ('section', 'len')), parts along dimension 3
- fluid_next: float32 [3, 8192], P(None, ('section', 'len', 'ht', 'wd')), parts along dimension 1
The draws below stay inside these ranges and needn't reach their ends.
There are 2 independent parts, one for each index of `section`. The reference program is written for one: setup_inputs(seed, part) draws one part's arguments, and reference() takes and returns one part's arrays. A program takes and returns all parts, laid end to end along the dimension named above; each array names one. Nothing has to cross between parts.
Inputs may be any that keep to these rules, and one draw needn't show every extreme that they name: `plan`: within the bins of one device no destination is named by more than 16 bins, and on some devices one is named by exactly 16. `counts`: about a third of the bins are full.
All inputs are finite; a program needn't handle non-finite values.
Results may differ from the reference program's by a relative error of at most 0.0003.
Values sent between devices are 32-bit elements; how exact they have to be, the bound alone decides.
A program may use at most 64 MiB of HBM per device.

```python
import math
import jax
import jax.numpy as jnp
import numpy as np
from jax import lax

GL = 8
GH = 2
GW = 2
SLOTS = 128
SUBSTEPS = 2
BINS_DEV = 32
CAP = 16
BL = 32
BH = 4
BW = 4
FCS = 1024
FCELLS = 4096
N_LEN = 4
N_HT = 2
N_WD = 2


def draw_counts(key, part):
    key = jax.random.fold_in(key, 11)
    raw = jax.random.randint(key, (BL, BH, BW), 0, SLOTS + SLOTS // 2)
    return jnp.minimum(raw, SLOTS).astype(jnp.int32)


def set_ends(values, key, low, high):
    spot = [jax.random.randint(jax.random.fold_in(key, axis), (), 0, length) for axis, length in enumerate(values.shape)]
    main_axis = values.shape.index(max(values.shape))
    beside = spot[:main_axis] + [(spot[main_axis] + 1) % values.shape[main_axis]] + spot[main_axis + 1:]
    return values.at[tuple(spot)].set(low).at[tuple(beside)].set(high)


def level_of(own_key, extent, cuts, low, top_value):
    factor_of = 1.0
    for axis_at, parts in cuts:
        steps = jax.random.uniform(jax.random.fold_in(jax.random.fold_in(own_key, 6), axis_at), (parts,), jnp.float32, low / len(cuts), top_value / len(cuts))
        factor_of = factor_of * jnp.repeat(jnp.exp(steps), extent[axis_at] // parts).reshape((-1,) + (1,) * (len(extent) - 1 - axis_at))
    return factor_of


def shared_out(key, own, number, rows, amount, top, limit, lean):
    order = jax.random.permutation(key, amount)
    heavy_load, common = load_shares(amount, rows * top, limit, lean, True), load_shares(amount, rows * top, limit, lean, False)
    places = jnp.arange(amount)

    def named(tallies, offset_by):
        used = int((tallies > 0).sum())
        fixed = max(1, used // 4)
        passed = fixed + (places - fixed + offset_by * (used - fixed)) % max(1, amount - fixed)
        return jnp.zeros((amount,), jnp.int32).at[order[jnp.where(places < fixed, places, passed)]].set(jnp.asarray(tallies, jnp.int32))

    tallies = jnp.where(number % 4 == 0, named(heavy_load, number // 4), named(common, number - number // 4 - 1))
    mixed = jax.random.permutation(jax.random.fold_in(own, 3), amount)
    donor, sink = mixed[0:amount // 2 * 2:2], mixed[1:amount // 2 * 2:2]
    room = jnp.minimum(tallies[donor] - 1, limit - tallies[sink]) // 2
    room = jnp.where((donor == order[0]) | (sink == order[0]) | (tallies[sink] == 0), 0, jnp.maximum(room, 0))
    passed = jax.random.randint(jax.random.fold_in(own, 4), (amount // 2,), 0, 1 << 20) % (room + 1)
    tallies = tallies.at[donor].add(-passed).at[sink].add(passed)
    labels = jnp.searchsorted(jnp.cumsum(tallies), jnp.arange(rows * top), side="right").astype(jnp.int32)
    grid = labels.reshape(top, rows).T
    grid = grid[jax.random.permutation(jax.random.fold_in(own, 1), rows)]
    offset_by = jax.random.randint(jax.random.fold_in(own, 2), (rows, 1), 0, top)
    return jnp.take_along_axis(grid, (jnp.arange(top)[None, :] + offset_by) % top, axis=1)


def load_shares(number_of, total, most, skew, full):
    weights = [(1 << 20) // math.isqrt(rank ** skew) + 1 for rank in range(1, number_of + 1)]
    largest = most if full else min(most, max(-(-total // number_of), total * weights[0] // sum(weights)))
    least = 1 if total - largest >= number_of - 1 else 0
    given, surplus = [largest] + [least] * (number_of - 1), total - largest - least * (number_of - 1)
    while surplus > 0:
        free = [i for i in range(1, number_of) if given[i] < largest] or [i for i in range(1, number_of) if given[i] < most]
        whole, left = sum([weights[i] for i in free]), surplus
        for i in free:
            more = min(most - given[i], max(1, left * weights[i] // whole), surplus)
            given[i] = given[i] + more
            surplus = surplus - more
    return np.array(given)


def scatter_about(rng, extent, width, limit, cuts=(), kind=jnp.bfloat16):
    level = level_of(rng, extent, cuts, -0.22, 0.18) if cuts else 1.0
    values = jax.random.normal(rng, extent, jnp.float32) * width * level
    return jnp.minimum(jnp.maximum(values, -limit), limit).astype(kind)


def setup_inputs(seed: int = 0, part: int = 0) -> dict:
    key_of = jax.random.split(jax.random.key(seed), 8)
    part_splits = jax.random.split(jax.random.fold_in(key_of[7], part), 8)
    positions = jnp.clip(1.0 * jax.random.uniform(part_splits[0], (3, BL, BH, BW, SLOTS), jnp.float32) ** level_of(part_splits[0], (3, BL, BH, BW, SLOTS), ((1, 4), (2, 2), (3, 2)), -0.2, 0.2), 0.0, 1.0)
    velocities = scatter_about(part_splits[1], (3, BL, BH, BW, SLOTS), 0.5, 3.0, ((1, 4), (2, 2), (3, 2)), jnp.float32)
    radius = jnp.clip(0.3 + 0.3 * jax.random.uniform(part_splits[2], (BL, BH, BW, SLOTS), jnp.float32) ** level_of(part_splits[2], (BL, BH, BW, SLOTS), ((0, 4), (1, 2), (2, 2)), -0.2, 0.2), 0.3, 0.6)
    counts = draw_counts(jax.random.fold_in(jax.random.fold_in(key_of[7], part), 71), part)
    cell_index = set_ends(jax.random.randint(part_splits[4], (BL, BH, BW, SLOTS), 0, FCS), jax.random.fold_in(part_splits[4], 1), 0, FCS - 1).astype(jnp.int32)
    fluid_velocity = scatter_about(part_splits[5], (3, FCELLS), 1.0, 6.0, ((1, 16),), jnp.float32)
    plan_keys = jax.random.split(jax.random.fold_in(part_splits[6], 1), N_LEN * N_HT * N_WD * BINS_DEV // BINS_DEV)
    plan_turns = jax.random.permutation(jax.random.fold_in(part_splits[6], 3), N_LEN * N_HT * N_WD * BINS_DEV // BINS_DEV)
    plan = jax.vmap(lambda own, number: shared_out(jax.random.fold_in(part_splits[6], 2), own, number, BINS_DEV, N_LEN, 1, CAP, 2))(plan_keys, plan_turns).reshape((N_LEN, N_HT, N_WD, BINS_DEV, 1))
    return dict(positions=positions, velocities=velocities, radius=radius, counts=counts, cell_index=cell_index, fluid_velocity=fluid_velocity, plan=plan)


STEP = 0.1
STIFF = 1.0
COUPLE = 0.5
RADIUS_REF = 0.45
OFFSETS = ((0, 0, 0), (1, 0, 0), (-1, 0, 0), (0, 1, 0), (0, -1, 0), (0, 0, 1), (0, 0, -1))


def contact_forces(padded):
    rows = padded.shape[1] - 2
    heights = padded.shape[2] - 2
    widths = padded.shape[3] - 2
    shifts = jnp.array(OFFSETS, dtype=jnp.float32).T.reshape(3, 7, 1, 1, 1)

    def one_row(index):
        slab = lax.dynamic_slice_in_dim(padded, index, 3, 1)
        centre = slab[:, 1, 1:heights + 1, 1:widths + 1, :]
        pieces = []
        for da, db, dc in OFFSETS:
            pieces.append(slab[:, 1 + da, 1 + db:1 + db + heights, 1 + dc:1 + dc + widths, :])
        sources = jnp.stack(pieces, axis=1)
        source_pos = sources[:3] + shifts
        diff = source_pos[:, :, :, :, None, :] - centre[:3][:, None, :, :, :, None]
        dist = jnp.sum(diff * diff, axis=0)
        reach = sources[3][:, :, :, None, :] + centre[3][None, :, :, :, None]
        weight = sources[4][:, :, :, None, :] * jnp.exp(-dist / (reach * reach))
        return -STIFF * jnp.sum(weight[None] * diff, axis=(1, 5))

    forces = lax.map(one_row, jnp.arange(rows, dtype=jnp.int32))
    return jnp.moveaxis(forces, 0, 1)


def pad_grid(field):
    return jnp.pad(field, ((0, 0), (1, 1), (1, 1), (1, 1), (0, 0)))


def reference(positions, velocities, radius, counts, cell_index, fluid_velocity, plan):
    live = (jnp.arange(SLOTS, dtype=jnp.int32)[None, None, None, :] < counts[..., None]).astype(jnp.float32)
    mass = (radius / RADIUS_REF) ** 3
    beta = radius
    slab = (jnp.arange(BL, dtype=jnp.int32) // GL).astype(jnp.int32)
    global_cell = (slab[:, None, None, None] * FCS + cell_index).astype(jnp.int32)
    fluid_here = fluid_velocity[:, global_cell]
    props = pad_grid(jnp.stack([radius, live]))
    place = positions
    speed = velocities
    acc = jnp.zeros_like(velocities)
    for step in range(SUBSTEPS):
        padded = jnp.concatenate([pad_grid(place), props], axis=0)
        force = contact_forces(padded)
        drag = beta * (fluid_here - speed)
        acc = acc + drag
        speed = speed + STEP * (force + drag) / mass
        place = place + STEP * speed
    term = jnp.concatenate([acc * live, (mass * live)[None]], axis=0)
    sums = jax.ops.segment_sum(term.reshape(4, -1).T, global_cell.reshape(-1), num_segments=FCELLS).T
    fluid_next = fluid_velocity - COUPLE * sums[:3] / (1.0 + sums[3:4])

    state = jnp.concatenate([place * live, speed * live, (radius * live)[None], live[None]], axis=0)
    state = state.reshape(8, N_LEN, GL, N_HT, GH, N_WD, GW, SLOTS)
    state = state.transpose(0, 3, 5, 1, 2, 4, 6, 7).reshape(8, N_HT, N_WD, N_LEN, BINS_DEV, SLOTS)
    dest = plan[..., 0].transpose(1, 2, 0, 3).astype(jnp.int32)
    order = jnp.arange(BINS_DEV, dtype=jnp.int32)
    same = dest[..., :, None] == dest[..., None, :]
    earlier = order[None, :] < order[:, None]
    rank = jnp.sum((same & earlier).astype(jnp.int32), axis=-1).astype(jnp.int32)
    source = jnp.arange(N_LEN, dtype=jnp.int32)[None, None, :, None]
    target = (dest * (N_LEN * CAP) + source * CAP + rank).astype(jnp.int32)
    hh = jnp.broadcast_to(jnp.arange(N_HT, dtype=jnp.int32)[:, None, None, None], target.shape)
    ww = jnp.broadcast_to(jnp.arange(N_WD, dtype=jnp.int32)[None, :, None, None], target.shape)
    moved = jnp.zeros((8, N_HT, N_WD, N_LEN * N_LEN * CAP, SLOTS), jnp.float32)
    moved = moved.at[:, hh, ww, target].set(state)
    return moved, fluid_next
```

```python
import functools
import math

import jax
import jax.numpy as jnp
from jax import lax
from jax.experimental import pallas as pl
from jax.experimental.pallas import tpu as pltpu
from jax.sharding import PartitionSpec as P

STEP = 0.1
COUPLE = 0.5
RADIUS_REF = 0.45
SCALE = math.sqrt(math.log2(math.e))
PARK = 64.0
MESH = pl.DeviceIdType.MESH
F32 = jnp.float32
BF16 = jnp.bfloat16


def dot(a, b):
    return jnp.dot(a, b, preferred_element_type=F32)


def dot_t(a, b):
    return lax.dot_general(a, b, (((1,), (1,)), ((), ())), preferred_element_type=F32)


def split3(x):
    h = x.astype(BF16).astype(F32)
    rest = x - h
    m = rest.astype(BF16).astype(F32)
    return h, m, rest - m


def axis_sides(axis, n, size):
    me = lax.axis_index(axis)
    if n == 1:
        return []
    if n == 2:
        return [(1 - me, (size - 1) * (1 - me), size * (1 - me) - me, None)]
    return [(me - 1, 0, -1, me > 0), (me + 1, size - 1, size, me < n - 1)]


def maybe(cond, fn):
    if cond is None:
        fn()
    else:
        pl.when(cond)(fn)


def kernel(
    nl, nh, nw, dims,
    pos_ref, vel_ref, rad_ref, cnt_ref, cell_ref, flu_ref, plan_ref,
    moved_ref, fnext_ref,
    xr, vr, ur, accr, lv, xp, hl, hh, hw, lt, rr, qq, gg, tc, oh, ft, pb, pr,
    out0, out1, out2, in0, in1, in2,
    halo_send, halo_recv, grp_send, grp_recv, a2a_send, a2a_recv,
):
    gl, gh, gw, cap, spread = dims
    bins = gl * gh * gw
    layer = gh * gw
    groups = nh * nw
    me_l = lax.axis_index("len")
    me_h = lax.axis_index("ht")
    me_w = lax.axis_index("wd")
    me_g = me_h * nw + me_w

    barrier = pltpu.get_barrier_semaphore()

    def len_peer(k):
        return lax.rem(me_l + k, nl)

    def grp_peer(k):
        return lax.rem(me_g + k, groups)

    def grp_id(k):
        g = grp_peer(k)
        return {"ht": g // nw, "wd": lax.rem(g, nw)}

    for k in range(1, nl):
        pl.semaphore_signal(barrier, inc=1, device_id={"len": len_peer(k)}, device_id_type=MESH)
    for k in range(1, groups):
        pl.semaphore_signal(barrier, inc=1, device_id=grp_id(k), device_id_type=MESH)

    row = lax.broadcasted_iota(jnp.int32, (8, 128), 0)
    lane = lax.broadcasted_iota(jnp.int32, (1, 128), 1)

    def load_layer(l, _):
        for h in range(gh):
            for w in range(gw):
                b = l * layer + h * gw + w
                xr[b] = jnp.zeros((8, 128), F32)
                vr[b] = jnp.zeros((8, 128), F32)
                for c in range(3):
                    xr[b, c : c + 1, :] = pos_ref[c, l, h, w : w + 1, :]
                    vr[b, c : c + 1, :] = vel_ref[c, l, h, w : w + 1, :]
                xr[b, 3:4, :] = rad_ref[l, h, w : w + 1, :]
                live = lane < cnt_ref[l, h, w]
                lv[b] = jnp.broadcast_to(jnp.where(live, 1.0, 0.0), (8, 128))
                xp[0, l, h, w] = jnp.where((lv[b] > 0.5) | (row >= 3), xr[b], PARK)
        return 0

    lax.fori_loop(0, gl, load_layer, 0)
    for c in range(3):
        for s in range(spread):
            ft[0, c * spread + s : c * spread + s + 1, :] = flu_ref[c : c + 1, s * 128 : (s + 1) * 128]
    for r_ in range(3 * spread, 8):
        ft[0, r_ : r_ + 1, :] = jnp.zeros((1, 128), F32)

    plans = []
    for axis, n, size, ref in (("len", nl, gl, hl), ("ht", nh, gh, hh), ("wd", nw, gw, hw)):
        plans.append((axis, ref, axis_sides(axis, n, size)))
    empty = jnp.where(row < 3, PARK, RADIUS_REF)
    for axis, ref, sides in plans:
        for s, (partner, face, coord, exists) in enumerate(sides):
            if exists is not None:

                def fill(ref=ref, s=s):
                    for t in range(2):
                        ref[t, s] = jnp.broadcast_to(empty, ref.shape[2:])

                pl.when(jnp.logical_not(exists))(fill)

    pl.semaphore_wait(barrier, nl - 1 + groups - 1)

    def halo_copies(t):
        res = []
        for a, (axis, ref, sides) in enumerate(plans):
            for s, (partner, face, coord, exists) in enumerate(sides):
                back = s if len(sides) == 1 else 1 - s
                src = (xp.at[t, face], xp.at[t, :, face], xp.at[t, :, :, face])[a]
                send = pltpu.make_async_remote_copy(
                    src_ref=src, dst_ref=ref.at[t, back],
                    send_sem=halo_send.at[t, a, s], recv_sem=halo_recv.at[t, a, back],
                    device_id={axis: partner}, device_id_type=MESH,
                )
                recv = pltpu.make_async_remote_copy(
                    src_ref=src, dst_ref=ref.at[t, s],
                    send_sem=halo_send.at[t, a, s], recv_sem=halo_recv.at[t, a, s],
                    device_id={axis: partner}, device_id_type=MESH,
                )
                res.append((send, recv, exists))
        return res

    def start_halo(t):
        for send, recv, exists in halo_copies(t):
            maybe(exists, send.start)

    def wait_halo(t):
        for send, recv, exists in halo_copies(t):
            maybe(exists, recv.wait_recv)

    def wait_halo_sent(t):
        for send, recv, exists in halo_copies(t):
            maybe(exists, send.wait_send)

    def grp_copies(phase):
        res = []
        for k in range(1, groups):
            src = ft.at[0] if phase == 0 else pb.at[grp_peer(k)]
            dst = ft.at[k] if phase == 0 else pr.at[k - 1]
            res.append(pltpu.make_async_remote_copy(
                src_ref=src, dst_ref=dst, send_sem=grp_send.at[phase, k - 1],
                recv_sem=grp_recv.at[phase, k - 1], device_id=grp_id(k), device_id_type=MESH))
        return res

    def a2a_copies(phase):
        src, dst = ((out0, in0), (out1, in1), (out2, in2))[phase]
        res = []
        for k in range(1, nl):
            res.append(pltpu.make_async_remote_copy(
                src_ref=src.at[len_peer(k)], dst_ref=dst.at[k - 1], send_sem=a2a_send.at[phase, k - 1],
                recv_sem=a2a_recv.at[phase, k - 1], device_id={"len": len_peer(k)}, device_id_type=MESH))
        return res

    start_halo(0)
    for copy in grp_copies(0):
        copy.start()

    dest = plan_ref[...]
    marks = jnp.where(dest == lax.broadcasted_iota(jnp.int32, (16, bins), 0), 1.0, 0.0)
    before = jnp.where(
        lax.broadcasted_iota(jnp.int32, (bins, bins), 0) < lax.broadcasted_iota(jnp.int32, (bins, bins), 1),
        1.0, 0.0)
    earlier = dot(marks.astype(BF16), before.astype(BF16))
    rank = jnp.sum(earlier * marks, axis=0, keepdims=True)
    slot = dest * cap + rank.astype(jnp.int32)
    sel = jnp.where(slot == lax.broadcasted_iota(jnp.int32, (nl * cap, bins), 0), 1.0, 0.0)
    sel3 = jnp.concatenate([sel, sel, sel], axis=1).astype(BF16)

    def pack(values, out, c):
        parts = jnp.concatenate(split3(values), axis=0).astype(BF16)
        got = dot(sel3, parts)
        for d in range(nl):
            out[d, c] = got[d * cap : (d + 1) * cap]

    alive = lv[:, 0, :]
    pack(xr[:, 3, :] * alive, out0, 0)
    pack(alive, out0, 1)
    for copy in a2a_copies(0):
        copy.start()

    mid = ((gl - 1) / 2 + 0.5, gh / 2, gw / 2)

    def coords(tile, where):
        off = jnp.zeros((8, 128), F32)
        for c in range(3):
            off = jnp.where(row == c, jnp.asarray(where[c], F32) - mid[c], off)
        return jnp.where(row < 3, (tile + off) * SCALE, 0.0)

    def right_side(t, index, tile, place):
        norm = jnp.sum(place * place, axis=0, keepdims=True)
        h, m, l = split3(jnp.where(row < 3, 2.0 * place, jnp.where(row == 3, 1.0, jnp.where(row == 4, norm, 0.0))))
        zero = jnp.zeros((8, 128), F32)
        left = jnp.concatenate([h, m, h, m, l, h, zero, zero], axis=0)
        rr[index, :, 0:128] = left.astype(BF16)
        if t == 0:
            rh, rm, rl = split3(tile[3:4])
            reach = jnp.where(row < 3, 1.0, jnp.where(row == 3, rh, jnp.where(row == 4, rm, jnp.where(row == 5, rl, 0.0))))
            right = jnp.concatenate([zero] * 6 + [reach, zero], axis=0)
            rr[index, :, 128:256] = right.astype(BF16)
        h, m, l = split3(jnp.where(row == 3, 1.0, place))
        q = jnp.concatenate([h + pltpu.roll(m, 4, 0), l], axis=0)
        qq[index] = jnp.concatenate([q, q], axis=1).astype(BF16)

    def left_side(index, tile, place):
        norm = jnp.sum(place * place, axis=0, keepdims=True)
        h, m, l = split3(jnp.where(row < 3, place, jnp.where(row == 3, -norm, jnp.where(row == 4, -1.0, 0.0))))
        rh, rm, rl = split3(tile[3:4])
        reach = jnp.where(row == 0, rh, jnp.where(row == 1, rm, jnp.where(row == 2, rl, jnp.where(row < 6, 1.0, 0.0))))
        zero = jnp.zeros((8, 128), F32)
        full = jnp.concatenate([h, h, m, m, h, l, reach, zero], axis=0)
        lt[index] = full.T.astype(BF16)

    def pair(t, i, j, block):
        if t == 0:
            both = dot(lt[i], rr[j])
            dist = both[:, :128]
            inv = pl.reciprocal(both[:, 128:], approx=False)
            inv = inv * inv
            tc[block] = inv
        else:
            dist = dot(lt[i], rr[j, :, 0:128])
            inv = tc[block]
        e = jnp.exp2(dist * inv)
        high = e.astype(BF16)
        low = (e - high.astype(F32)).astype(BF16)
        return high, low

    def onto_j(i, e):
        return dot(qq[i], jnp.concatenate(e, axis=0))

    def onto_i(j, e):
        return dot_t(qq[j], jnp.concatenate(e, axis=1))

    ht_pairs = [(h * gw + w, (h + 1) * gw + w) for h in range(gh - 1) for w in range(gw)]
    wd_pairs = [(h * gw + w, h * gw + w + 1) for h in range(gh) for w in range(gw - 1)]
    in_layer = ht_pairs + wd_pairs
    per_layer = layer + len(in_layer)
    base_len = gl * per_layer
    base_halo = base_len + (gl - 1) * layer

    def prepare(t):
        def one(l, _):
            for h in range(gh):
                for w in range(gw):
                    b = l * layer + h * gw + w
                    tile = xp[t, l, h, w]
                    place = coords(tile, (l, h, w))
                    right_side(t, b, tile, place)
                    left_side(b, tile, place)
            return 0

        lax.fori_loop(0, gl, one, 0)

    def interior(t):
        def one(l, _):
            base = l * layer
            sums = [None] * layer
            for n_ in range(layer):
                sums[n_] = onto_j(base + n_, pair(t, base + n_, base + n_, l * per_layer + n_))
            for n_, (i, j) in enumerate(in_layer):
                e = pair(t, base + i, base + j, l * per_layer + layer + n_)
                sums[j] = sums[j] + onto_j(base + i, e)
                sums[i] = sums[i] + onto_i(base + j, e)
            for n_ in range(layer):
                gg[base + n_] = sums[n_]
            return 0

        lax.fori_loop(0, gl, one, 0)

        def along(l, _):
            base = l * layer
            ups, downs = [], []
            for n_ in range(layer):
                e = pair(t, base + n_, base + layer + n_, base_len + base + n_)
                ups.append(onto_j(base + n_, e))
                downs.append(onto_i(base + layer + n_, e))
            for n_ in range(layer):
                gg[base + n_] += downs[n_]
                gg[base + layer + n_] += ups[n_]
            return 0

        lax.fori_loop(0, gl - 1, along, 0)

    def boundary(t):
        at = bins
        for s, (partner, face, coord, exists) in enumerate(plans[0][2]):
            sums = []
            for h in range(gh):
                for w in range(gw):
                    tile = hl[t, s, h, w]
                    right_side(t, at + h * gw + w, tile, coords(tile, (coord, h, w)))
            for n_ in range(layer):
                e = pair(t, face * layer + n_, at + n_, base_halo + at - bins + n_)
                sums.append(onto_i(at + n_, e))
            for n_ in range(layer):
                gg[face * layer + n_] += sums[n_]
            at += layer
        for a, across in ((1, gw), (2, gh)):
            ref = plans[a][1]
            for s, (partner, face, coord, exists) in enumerate(plans[a][2]):

                def one(l, _, ref=ref, s=s, face=face, coord=coord, a=a, across=across, at=at):
                    targets, sums = [], []
                    for y in range(across):
                        tile = ref[t, s, l, y]
                        place = coords(tile, (l, coord, y) if a == 1 else (l, y, coord))
                        right_side(t, at + l * across + y, tile, place)
                    for y in range(across):
                        n_ = at + l * across + y
                        target = l * layer + (face * gw + y if a == 1 else y * gw + face)
                        e = pair(t, target, n_, base_halo + n_ - bins)
                        targets.append(target)
                        sums.append(onto_i(n_, e))
                    for target, got in zip(targets, sums):
                        gg[target] += got
                    return 0

                lax.fori_loop(0, gl, one, 0)
                at += gl * across

    lo_rows = lax.broadcasted_iota(jnp.int32, (128, 128), 0)

    def hi_mask(cells, g):
        return lax.shift_right_logical(cells, 7) == g * spread + lax.rem(row, spread)

    def read_fluid():
        for copy in grp_copies(0):
            copy.wait_recv()
        table = []
        for k in range(groups):
            table.append(ft[k])
        table = jnp.concatenate(table, axis=0)
        table = jnp.concatenate(split3(table), axis=0).astype(BF16)

        def one(l, _):
            for h in range(gh):
                for w in range(gw):
                    n_ = h * gw + w
                    cells = cell_ref[l, h, w : w + 1, :]
                    low = lax.rem(cells, 128)
                    oh[l, :, n_ * 128 : (n_ + 1) * 128] = jnp.where(low == lo_rows, 1.0, 0.0).astype(BF16)
            got = dot(table, oh[l])
            full = got[: groups * 8] + got[groups * 8 : groups * 16] + got[groups * 16 :]
            for h in range(gh):
                for w in range(gw):
                    n_ = h * gw + w
                    cells = cell_ref[l, h, w : w + 1, :]
                    mine = full[:, n_ * 128 : (n_ + 1) * 128]
                    u = jnp.zeros((8, 128), F32)
                    for k in range(groups):
                        g = lax.rem(me_g - k + groups, groups)
                        u = u + jnp.where(hi_mask(cells, g), mine[k * 8 : (k + 1) * 8], 0.0)
                    b = l * layer + n_
                    ur[b] = jnp.zeros((8, 128), F32)
                    for c in range(3):
                        ur[b, c : c + 1, :] = jnp.sum(u[c * spread : (c + 1) * spread], axis=0, keepdims=True)
            return 0

        lax.fori_loop(0, gl, one, 0)

    def update(t):
        def one(l, _):
            for h in range(gh):
                for w in range(gw):
                    b = l * layer + h * gw + w
                    tile = xr[b]
                    radius = tile[3:4]
                    ratio = radius * (1.0 / RADIUS_REF)
                    mass = ratio * ratio * ratio
                    place = coords(xp[t, l, h, w], (l, h, w))
                    g = gg[b]
                    total = g[:8] + pltpu.roll(g[:8], 4, 0) + g[8:]
                    force = (place * total[3:4] - total) * (1.0 / SCALE)
                    speed = vr[b]
                    drag = radius * (ur[b] - speed)
                    accr[b] = drag if t == 0 else accr[b] + drag
                    speed = speed + STEP * (force + drag) * (1.0 / mass)
                    alive = lv[b] > 0.5
                    speed = jnp.where((row < 3) & alive, speed, 0.0)
                    vr[b] = speed
                    if t == 0:
                        tile = tile + STEP * speed
                        xr[b] = tile
                        xp[1, l, h, w] = jnp.where(alive | (row >= 3), tile, PARK)
            return 0

        lax.fori_loop(0, gl, one, 0)

    prepare(0)
    interior(0)
    read_fluid()
    wait_halo(0)
    boundary(0)
    update(0)
    start_halo(1)
    for c in range(3):
        pack(xr[:, c, :] * alive, out1, c)
    for copy in a2a_copies(1):
        copy.start()

    prepare(1)
    interior(1)
    wait_halo(1)
    boundary(1)
    update(1)
    for c in range(3):
        pack(vr[:, c, :], out2, c)
    for copy in a2a_copies(2):
        copy.start()

    def cell_sums(l, total):
        lefts = []
        for h in range(gh):
            for w in range(gw):
                b = l * layer + h * gw + w
                cells = cell_ref[l, h, w : w + 1, :]
                radius = xr[b, 3:4, :]
                ratio = radius * (1.0 / RADIUS_REF)
                live_row = lv[b, 0:1, :]
                rows = [accr[b, c : c + 1, :] * live_row for c in range(3)] + [ratio * ratio * ratio * live_row]
                term = jnp.concatenate([rows[r_ // spread] for r_ in range(4 * spread)], axis=0)
                parts = split3(term)
                pieces = []
                for part in parts:
                    for g in range(groups):
                        pieces.append(jnp.where(hi_mask(cells, g), part, 0.0))
                lefts.append(jnp.concatenate(pieces, axis=0).astype(BF16))
        return total + dot_t(jnp.concatenate(lefts, axis=1), oh[l])

    sums = lax.fori_loop(0, gl, cell_sums, jnp.zeros((groups * 24, 128), F32))
    sums = sums[: groups * 8] + sums[groups * 8 : groups * 16] + sums[groups * 16 :]
    for g in range(groups):
        pb[g] = sums[g * 8 : (g + 1) * 8]
    for copy in grp_copies(1):
        copy.start()

    def landed(own, arrived, c, put):
        put(me_l, own[me_l, c])
        for k in range(1, nl):
            put(lax.rem(me_l - k + nl, nl), arrived[k - 1, c])

    for copy in a2a_copies(0) + a2a_copies(1):
        copy.wait_recv()
    for k in range(nl):
        source = lax.rem(me_l - k + nl, nl)
        at = pl.ds(source * cap, cap)
        early = out0.at[me_l] if k == 0 else in0.at[k - 1]
        for c in range(2):
            moved_ref[6 + c, at, :] = early[c]

    for copy in grp_copies(1):
        copy.wait_recv()
    whole = pb[me_g]
    for k in range(groups - 1):
        whole = whole + pr[k]
    mass_rows = whole[3 * spread : 4 * spread]
    for c in range(3):
        ratio = whole[c * spread : (c + 1) * spread] / (1.0 + mass_rows)
        fresh = ft[0, c * spread : (c + 1) * spread, :] - COUPLE * ratio
        for s in range(spread):
            fnext_ref[c : c + 1, s * 128 : (s + 1) * 128] = fresh[s : s + 1]

    for copy in a2a_copies(2):
        copy.wait_recv()
    for k in range(nl):
        source = lax.rem(me_l - k + nl, nl)
        at = pl.ds(source * cap, cap)
        place = out1.at[me_l] if k == 0 else in1.at[k - 1]
        speed = out2.at[me_l] if k == 0 else in2.at[k - 1]
        for c in range(3):
            v = speed[c]
            moved_ref[3 + c, at, :] = v
            moved_ref[c, at, :] = place[c] + STEP * v

    for t in range(2):
        wait_halo_sent(t)
        for copy in grp_copies(t):
            copy.wait_send()
    for phase in range(3):
        for copy in a2a_copies(phase):
            copy.wait_send()


def per_device(nl, nh, nw, positions, velocities, radius, counts, cell_index, fluid_velocity, plan):
    gl, gh, gw, slots = radius.shape
    bins = gl * gh * gw
    cap = max(2, 2 * bins // nl)
    spread = fluid_velocity.shape[1] // 128
    groups = nh * nw
    dims = (gl, gh, gw, cap, spread)

    def count(n):
        return 1 if n <= 2 else 2

    sl, sh, sw = count(nl), count(nh), count(nw)
    halos = sl * gh * gw + sh * gl * gw + sw * gl * gh
    blocks = gl * (gh * gw + (gh - 1) * gw + gh * (gw - 1)) + (gl - 1) * gh * gw + halos
    vmem = pltpu.VMEM
    scratch = [
        vmem((bins, 8, 128), F32), vmem((bins, 8, 128), F32), vmem((bins, 8, 128), F32),
        vmem((bins, 8, 128), F32), vmem((bins, 8, 128), F32),
        vmem((2, gl, gh, gw, 8, 128), F32),
        vmem((2, sl, gh, gw, 8, 128), F32), vmem((2, sh, gl, gw, 8, 128), F32), vmem((2, sw, gl, gh, 8, 128), F32),
        vmem((bins, 128, 64), BF16), vmem((bins + halos, 64, 256), BF16), vmem((bins + halos, 16, 256), BF16),
        vmem((bins, 16, 128), F32), vmem((blocks, 128, 128), F32),
        vmem((gl, 128, gh * gw * 128), BF16),
        vmem((groups, 8, 128), F32), vmem((groups, 8, 128), F32), vmem((max(1, groups - 1), 8, 128), F32),
        vmem((nl, 2, cap, 128), F32), vmem((nl, 3, cap, 128), F32), vmem((nl, 3, cap, 128), F32),
        vmem((nl - 1, 2, cap, 128), F32), vmem((nl - 1, 3, cap, 128), F32), vmem((nl - 1, 3, cap, 128), F32),
        pltpu.SemaphoreType.DMA((2, 3, 2)), pltpu.SemaphoreType.DMA((2, 3, 2)),
        pltpu.SemaphoreType.DMA((2, groups)), pltpu.SemaphoreType.DMA((2, groups)),
        pltpu.SemaphoreType.DMA((3, nl)), pltpu.SemaphoreType.DMA((3, nl)),
    ]
    in_vmem = pl.BlockSpec(memory_space=pltpu.VMEM)
    in_smem = pl.BlockSpec(memory_space=pltpu.SMEM)
    moved, fluid_next = pl.pallas_call(
        functools.partial(kernel, nl, nh, nw, dims),
        out_shape=(
            jax.ShapeDtypeStruct((8, nl * cap, slots), F32),
            jax.ShapeDtypeStruct(fluid_velocity.shape, F32),
        ),
        in_specs=[in_vmem, in_vmem, in_vmem, in_smem, in_vmem, in_vmem, in_vmem],
        out_specs=(in_vmem, in_vmem),
        scratch_shapes=scratch,
        compiler_params=pltpu.CompilerParams(
            collective_id=0, has_side_effects=True, vmem_limit_bytes=48 * 1024 * 1024
        ),
    )(positions, velocities, radius, counts, cell_index, fluid_velocity, plan.reshape(1, bins))
    return moved.reshape(8, 1, 1, nl * cap, slots), fluid_next


def solution(mesh):
    sizes = dict(mesh.shape)
    in_specs = (
        P(None, ("section", "len"), "ht", "wd", None),
        P(None, ("section", "len"), "ht", "wd", None),
        P(("section", "len"), "ht", "wd", None),
        P(("section", "len"), "ht", "wd"),
        P(("section", "len"), "ht", "wd", None),
        P(None, ("section", "len", "ht", "wd")),
        P(("section", "len"), "ht", "wd", None, None),
    )
    out_specs = (
        P(None, "ht", "wd", ("section", "len"), None),
        P(None, ("section", "len", "ht", "wd")),
    )
    body = functools.partial(per_device, sizes["len"], sizes["ht"], sizes["wd"])
    return jax.shard_map(body, mesh=mesh, in_specs=in_specs, out_specs=out_specs, check_vma=False)
```

```python
import functools

import jax
import jax.numpy as jnp
from jax import lax
from jax.experimental import pallas as pl
from jax.experimental.pallas import tpu as pltpu
from jax.sharding import PartitionSpec as P

STEP = 0.1
COUPLE = 0.5
RADIUS_REF = 0.45
PARK = 64.0
MESH = pl.DeviceIdType.MESH
F32 = jnp.float32
BF16 = jnp.bfloat16


def dot(a, b):
    return jnp.dot(a, b, preferred_element_type=F32)


def dot_t(a, b):
    return lax.dot_general(a, b, (((1,), (1,)), ((), ())), preferred_element_type=F32)


def split3(x):
    h = x.astype(BF16).astype(F32)
    rest = x - h
    m = rest.astype(BF16).astype(F32)
    return h, m, rest - m


def axis_sides(axis, n, size):
    me = lax.axis_index(axis)
    if n == 1:
        return []
    if n == 2:
        return [(1 - me, (size - 1) * (1 - me), size * (1 - me) - me, None)]
    return [(me - 1, 0, -1, me > 0), (me + 1, size - 1, size, me < n - 1)]


def maybe(cond, fn):
    if cond is None:
        fn()
    else:
        pl.when(cond)(fn)


def kernel(
    nl, nh, nw, dims,
    pos_ref, vel_ref, rad_ref, cnt_ref, cell_ref, flu_ref, plan_ref,
    moved_ref, fnext_ref,
    xr, vr, ur, accr, lv, xp, hl, hh, hw, lt, rr, pc, gg, tc, oh, ft, pb, pr,
    out0, out1, out2, in0, in1, in2,
    halo_send, halo_recv, grp_send, grp_recv, a2a_send, a2a_recv,
):
    gl, gh, gw, cap, spread = dims
    bins = gl * gh * gw
    layer = gh * gw
    groups = nh * nw
    me_l = lax.axis_index("len")
    me_h = lax.axis_index("ht")
    me_w = lax.axis_index("wd")
    me_g = me_h * nw + me_w

    barrier = pltpu.get_barrier_semaphore()

    def len_peer(k):
        return lax.rem(me_l + k, nl)

    def grp_peer(k):
        return lax.rem(me_g + k, groups)

    def grp_id(k):
        g = grp_peer(k)
        return {"ht": g // nw, "wd": lax.rem(g, nw)}

    for k in range(1, nl):
        pl.semaphore_signal(barrier, inc=1, device_id={"len": len_peer(k)}, device_id_type=MESH)
    for k in range(1, groups):
        pl.semaphore_signal(barrier, inc=1, device_id=grp_id(k), device_id_type=MESH)

    row = lax.broadcasted_iota(jnp.int32, (8, 128), 0)
    lane = lax.broadcasted_iota(jnp.int32, (1, 128), 1)

    def load_layer(l, _):
        for h in range(gh):
            for w in range(gw):
                b = l * layer + h * gw + w
                xr[b] = jnp.zeros((8, 128), F32)
                vr[b] = jnp.zeros((8, 128), F32)
                for c in range(3):
                    xr[b, c : c + 1, :] = pos_ref[c, l, h, w : w + 1, :]
                    vr[b, c : c + 1, :] = vel_ref[c, l, h, w : w + 1, :]
                xr[b, 3:4, :] = rad_ref[l, h, w : w + 1, :]
                live = lane < cnt_ref[l, h, w]
                lv[b] = jnp.broadcast_to(jnp.where(live, 1.0, 0.0), (8, 128))
                xp[0, l, h, w] = jnp.where((lv[b] > 0.5) | (row >= 3), xr[b], PARK)
        return 0

    lax.fori_loop(0, gl, load_layer, 0)
    for c in range(3):
        for s in range(spread):
            ft[0, c * spread + s : c * spread + s + 1, :] = flu_ref[c : c + 1, s * 128 : (s + 1) * 128]
    for r_ in range(3 * spread, 8):
        ft[0, r_ : r_ + 1, :] = jnp.zeros((1, 128), F32)

    plans = []
    for axis, n, size, ref in (("len", nl, gl, hl), ("ht", nh, gh, hh), ("wd", nw, gw, hw)):
        plans.append((axis, ref, axis_sides(axis, n, size)))
    empty = jnp.where(row < 3, PARK, RADIUS_REF)
    for axis, ref, sides in plans:
        for s, (partner, face, coord, exists) in enumerate(sides):
            if exists is not None:

                def fill(ref=ref, s=s):
                    for t in range(2):
                        ref[t, s] = jnp.broadcast_to(empty, ref.shape[2:])

                pl.when(jnp.logical_not(exists))(fill)

    pl.semaphore_wait(barrier, nl - 1 + groups - 1)

    def halo_copies(t):
        res = []
        for a, (axis, ref, sides) in enumerate(plans):
            for s, (partner, face, coord, exists) in enumerate(sides):
                back = s if len(sides) == 1 else 1 - s
                src = (xp.at[t, face], xp.at[t, :, face], xp.at[t, :, :, face])[a]
                send = pltpu.make_async_remote_copy(
                    src_ref=src, dst_ref=ref.at[t, back],
                    send_sem=halo_send.at[t, a, s], recv_sem=halo_recv.at[t, a, back],
                    device_id={axis: partner}, device_id_type=MESH,
                )
                recv = pltpu.make_async_remote_copy(
                    src_ref=src, dst_ref=ref.at[t, s],
                    send_sem=halo_send.at[t, a, s], recv_sem=halo_recv.at[t, a, s],
                    device_id={axis: partner}, device_id_type=MESH,
                )
                res.append((send, recv, exists))
        return res

    def start_halo(t):
        for send, recv, exists in halo_copies(t):
            maybe(exists, send.start)

    def wait_halo(t):
        for send, recv, exists in halo_copies(t):
            maybe(exists, recv.wait_recv)

    def wait_halo_sent(t):
        for send, recv, exists in halo_copies(t):
            maybe(exists, send.wait_send)

    def grp_copies(phase):
        res = []
        for k in range(1, groups):
            src = ft.at[0] if phase == 0 else pb.at[grp_peer(k)]
            dst = ft.at[k] if phase == 0 else pr.at[k - 1]
            res.append(pltpu.make_async_remote_copy(
                src_ref=src, dst_ref=dst, send_sem=grp_send.at[phase, k - 1],
                recv_sem=grp_recv.at[phase, k - 1], device_id=grp_id(k), device_id_type=MESH))
        return res

    def a2a_copies(phase):
        src, dst = ((out0, in0), (out1, in1), (out2, in2))[phase]
        res = []
        for k in range(1, nl):
            res.append(pltpu.make_async_remote_copy(
                src_ref=src.at[len_peer(k)], dst_ref=dst.at[k - 1], send_sem=a2a_send.at[phase, k - 1],
                recv_sem=a2a_recv.at[phase, k - 1], device_id={"len": len_peer(k)}, device_id_type=MESH))
        return res

    start_halo(0)
    for copy in grp_copies(0):
        copy.start()

    dest = plan_ref[...]
    marks = jnp.where(dest == lax.broadcasted_iota(jnp.int32, (16, bins), 0), 1.0, 0.0)
    before = jnp.where(
        lax.broadcasted_iota(jnp.int32, (bins, bins), 0) < lax.broadcasted_iota(jnp.int32, (bins, bins), 1),
        1.0, 0.0)
    earlier = dot(marks.astype(BF16), before.astype(BF16))
    rank = jnp.sum(earlier * marks, axis=0, keepdims=True)
    slot = dest * cap + rank.astype(jnp.int32)
    sel = jnp.where(slot == lax.broadcasted_iota(jnp.int32, (nl * cap, bins), 0), 1.0, 0.0)
    sel3 = jnp.concatenate([sel, sel, sel], axis=1).astype(BF16)

    def pack(values, out, c):
        parts = jnp.concatenate(split3(values), axis=0).astype(BF16)
        got = dot(sel3, parts)
        for d in range(nl):
            out[d, c] = got[d * cap : (d + 1) * cap]

    alive = lv[:, 0, :]
    pack(xr[:, 3, :] * alive, out0, 0)
    pack(alive, out0, 1)
    for copy in a2a_copies(0):
        copy.start()

    mid = ((gl - 1) / 2 + 0.5, gh / 2, gw / 2)

    def coords(tile, where):
        off = jnp.zeros((8, 128), F32)
        for c in range(3):
            off = jnp.where(row == c, jnp.asarray(where[c], F32) - mid[c], off)
        return jnp.where(row < 3, tile + off, 0.0)

    zero = jnp.zeros((8, 128), F32)
    part_row = lax.broadcasted_iota(jnp.int32, (64, 384), 0)
    part_of = part_row // 8
    spread_out = jnp.where(
        (lax.rem(part_row, 8) == lax.broadcasted_iota(jnp.int32, (64, 384), 1) // 128)
        & ((part_of == 0) | (part_of == 2) | (part_of == 5)),
        1.0, 0.0).astype(BF16)

    def right_side(t, index, tile, place):
        norm = jnp.sum(place * place, axis=0, keepdims=True)
        h, m, l = split3(jnp.where(row < 3, 2.0 * place, jnp.where(row == 3, 1.0, jnp.where(row == 4, norm, 0.0))))
        left = jnp.concatenate([h, m, h, m, l, h, zero, zero], axis=0)
        rr[index, :, 0:128] = left.astype(BF16)
        if t == 0:
            rh, rm, rl = split3(tile[3:4])
            reach = jnp.where(row < 3, 1.0, jnp.where(row == 3, rh, jnp.where(row == 4, rm, jnp.where(row == 5, rl, 0.0))))
            right = jnp.concatenate([zero] * 6 + [reach, zero], axis=0)
            rr[index, :, 128:256] = right.astype(BF16)

    def left_side(index, tile, place):
        norm = jnp.sum(place * place, axis=0, keepdims=True)
        h, m, l = split3(jnp.where(row < 3, place, jnp.where(row == 3, -norm, jnp.where(row == 4, -1.0, 0.0))))
        rh, rm, rl = split3(tile[3:4])
        reach = jnp.where(row == 0, rh, jnp.where(row == 1, rm, jnp.where(row == 2, rl, jnp.where(row < 6, 1.0, 0.0))))
        full = jnp.concatenate([h, h, m, m, h, l, reach, zero], axis=0)
        left = full.T.astype(BF16)
        lt[index] = left
        pc[index] = dot(left, spread_out)

    def push(t, target, source, block):
        if t == 0:
            both = dot(lt[source], rr[target])
            dist = both[:, :128]
            inv = pl.reciprocal(both[:, 128:], approx=False)
            inv = inv * inv
            tc[block] = inv
        else:
            dist = dot(lt[source], rr[target, :, 0:128])
            inv = tc[block]
        e = jnp.exp(dist * inv)
        acc = [None] * 4
        for k in range(16):
            piece = e[8 * k : 8 * k + 8]
            terms = [piece * pc[source, 8 * k : 8 * k + 8, 128 * c : 128 * c + 128] for c in range(3)] + [piece]
            acc = terms if k == 0 else [a + b for a, b in zip(acc, terms)]
        return jnp.concatenate(acc, axis=0)

    near = []
    for h in range(gh):
        for w in range(gw):
            near.append((h * gw + w, h * gw + w))
            for h2, w2 in ((h - 1, w), (h + 1, w), (h, w - 1), (h, w + 1)):
                if 0 <= h2 < gh and 0 <= w2 < gw:
                    near.append((h * gw + w, h2 * gw + w2))
    per_layer = len(near)
    base_len = gl * per_layer
    base_halo = base_len + 2 * (gl - 1) * layer

    def prepare(t):
        def one(l, _):
            for h in range(gh):
                for w in range(gw):
                    b = l * layer + h * gw + w
                    tile = xp[t, l, h, w]
                    place = coords(tile, (l, h, w))
                    right_side(t, b, tile, place)
                    left_side(b, tile, place)
            return 0

        lax.fori_loop(0, gl, one, 0)

    def interior(t):
        def one(l, _):
            base = l * layer
            sums = [None] * layer
            for n_, (i, j) in enumerate(near):
                got = push(t, base + i, base + j, l * per_layer + n_)
                sums[i] = got if sums[i] is None else sums[i] + got
            for n_ in range(layer):
                gg[base + n_] = sums[n_]
            return 0

        lax.fori_loop(0, gl, one, 0)

        def along(l, _):
            base = l * layer
            ups, downs = [], []
            for n_ in range(layer):
                block = base_len + 2 * (base + n_)
                ups.append(push(t, base + layer + n_, base + n_, block))
                downs.append(push(t, base + n_, base + layer + n_, block + 1))
            for n_ in range(layer):
                gg[base + n_] += downs[n_]
                gg[base + layer + n_] += ups[n_]
            return 0

        lax.fori_loop(0, gl - 1, along, 0)

    def boundary(t):
        at = bins
        for s, (partner, face, coord, exists) in enumerate(plans[0][2]):
            sums = []
            for h in range(gh):
                for w in range(gw):
                    tile = hl[t, s, h, w]
                    left_side(at + h * gw + w, tile, coords(tile, (coord, h, w)))
            for n_ in range(layer):
                sums.append(push(t, face * layer + n_, at + n_, base_halo + at - bins + n_))
            for n_ in range(layer):
                gg[face * layer + n_] += sums[n_]
            at += layer
        for a, across in ((1, gw), (2, gh)):
            ref = plans[a][1]
            for s, (partner, face, coord, exists) in enumerate(plans[a][2]):
                step = 2 if gl % 2 == 0 else 1

                def one(p, _, ref=ref, s=s, face=face, coord=coord, a=a, across=across, at=at, step=step):
                    targets, sums = [], []
                    for q in range(step):
                        l = p * step + q
                        for y in range(across):
                            tile = ref[t, s, l, y]
                            place = coords(tile, (l, coord, y) if a == 1 else (l, y, coord))
                            left_side(at + l * across + y, tile, place)
                    for q in range(step):
                        l = p * step + q
                        for y in range(across):
                            n_ = at + l * across + y
                            target = l * layer + (face * gw + y if a == 1 else y * gw + face)
                            targets.append(target)
                            sums.append(push(t, target, n_, base_halo + n_ - bins))
                    for target, got in zip(targets, sums):
                        gg[target] += got
                    return 0

                lax.fori_loop(0, gl // step, one, 0)
                at += gl * across

    lo_rows = lax.broadcasted_iota(jnp.int32, (128, 128), 0)

    def hi_mask(cells, g):
        return lax.shift_right_logical(cells, 7) == g * spread + lax.rem(row, spread)

    def read_fluid():
        for copy in grp_copies(0):
            copy.wait_recv()
        table = []
        for k in range(groups):
            table.append(ft[k])
        table = jnp.concatenate(table, axis=0)
        table = jnp.concatenate(split3(table), axis=0).astype(BF16)

        def one(l, _):
            for h in range(gh):
                for w in range(gw):
                    n_ = h * gw + w
                    cells = cell_ref[l, h, w : w + 1, :]
                    low = lax.rem(cells, 128)
                    oh[l, :, n_ * 128 : (n_ + 1) * 128] = jnp.where(low == lo_rows, 1.0, 0.0).astype(BF16)
            got = dot(table, oh[l])
            full = got[: groups * 8] + got[groups * 8 : groups * 16] + got[groups * 16 :]
            for h in range(gh):
                for w in range(gw):
                    n_ = h * gw + w
                    cells = cell_ref[l, h, w : w + 1, :]
                    mine = full[:, n_ * 128 : (n_ + 1) * 128]
                    u = jnp.zeros((8, 128), F32)
                    for k in range(groups):
                        g = lax.rem(me_g - k + groups, groups)
                        u = u + jnp.where(hi_mask(cells, g), mine[k * 8 : (k + 1) * 8], 0.0)
                    b = l * layer + n_
                    ur[b] = jnp.zeros((8, 128), F32)
                    for c in range(3):
                        ur[b, c : c + 1, :] = jnp.sum(u[c * spread : (c + 1) * spread], axis=0, keepdims=True)
            return 0

        lax.fori_loop(0, gl, one, 0)

    def update(t):
        def one(l, _):
            for h in range(gh):
                for w in range(gw):
                    b = l * layer + h * gw + w
                    tile = xr[b]
                    radius = tile[3:4]
                    ratio = radius * (1.0 / RADIUS_REF)
                    mass = ratio * ratio * ratio
                    place = coords(xp[t, l, h, w], (l, h, w))
                    g = gg[b]
                    rows = [jnp.sum(g[8 * c : 8 * c + 8], axis=0, keepdims=True) for c in range(4)]
                    total = jnp.concatenate(rows + rows, axis=0)
                    force = place * rows[3] - total
                    speed = vr[b]
                    drag = radius * (ur[b] - speed)
                    accr[b] = drag if t == 0 else accr[b] + drag
                    speed = speed + STEP * (force + drag) * (1.0 / mass)
                    alive = lv[b] > 0.5
                    speed = jnp.where((row < 3) & alive, speed, 0.0)
                    vr[b] = speed
                    if t == 0:
                        tile = tile + STEP * speed
                        xr[b] = tile
                        xp[1, l, h, w] = jnp.where(alive | (row >= 3), tile, PARK)
            return 0

        lax.fori_loop(0, gl, one, 0)

    prepare(0)
    interior(0)
    read_fluid()
    wait_halo(0)
    boundary(0)
    update(0)
    start_halo(1)
    for c in range(3):
        pack(xr[:, c, :] * alive, out1, c)
    for copy in a2a_copies(1):
        copy.start()

    prepare(1)
    interior(1)
    wait_halo(1)
    boundary(1)
    update(1)
    for c in range(3):
        pack(vr[:, c, :], out2, c)
    for copy in a2a_copies(2):
        copy.start()

    def cell_sums(l, total):
        lefts = []
        for h in range(gh):
            for w in range(gw):
                b = l * layer + h * gw + w
                cells = cell_ref[l, h, w : w + 1, :]
                radius = xr[b, 3:4, :]
                ratio = radius * (1.0 / RADIUS_REF)
                live_row = lv[b, 0:1, :]
                rows = [accr[b, c : c + 1, :] * live_row for c in range(3)] + [ratio * ratio * ratio * live_row]
                term = jnp.concatenate([rows[r_ // spread] for r_ in range(4 * spread)], axis=0)
                parts = split3(term)
                pieces = []
                for part in parts:
                    for g in range(groups):
                        pieces.append(jnp.where(hi_mask(cells, g), part, 0.0))
                lefts.append(jnp.concatenate(pieces, axis=0).astype(BF16))
        return total + dot_t(jnp.concatenate(lefts, axis=1), oh[l])

    sums = lax.fori_loop(0, gl, cell_sums, jnp.zeros((groups * 24, 128), F32))
    sums = sums[: groups * 8] + sums[groups * 8 : groups * 16] + sums[groups * 16 :]
    for g in range(groups):
        pb[g] = sums[g * 8 : (g + 1) * 8]
    for copy in grp_copies(1):
        copy.start()

    def landed(own, arrived, c, put):
        put(me_l, own[me_l, c])
        for k in range(1, nl):
            put(lax.rem(me_l - k + nl, nl), arrived[k - 1, c])

    for copy in a2a_copies(0) + a2a_copies(1):
        copy.wait_recv()
    for k in range(nl):
        source = lax.rem(me_l - k + nl, nl)
        at = pl.ds(source * cap, cap)
        early = out0.at[me_l] if k == 0 else in0.at[k - 1]
        for c in range(2):
            moved_ref[6 + c, at, :] = early[c]

    for copy in grp_copies(1):
        copy.wait_recv()
    whole = pb[me_g]
    for k in range(groups - 1):
        whole = whole + pr[k]
    mass_rows = whole[3 * spread : 4 * spread]
    for c in range(3):
        ratio = whole[c * spread : (c + 1) * spread] / (1.0 + mass_rows)
        fresh = ft[0, c * spread : (c + 1) * spread, :] - COUPLE * ratio
        for s in range(spread):
            fnext_ref[c : c + 1, s * 128 : (s + 1) * 128] = fresh[s : s + 1]

    for copy in a2a_copies(2):
        copy.wait_recv()
    for k in range(nl):
        source = lax.rem(me_l - k + nl, nl)
        at = pl.ds(source * cap, cap)
        place = out1.at[me_l] if k == 0 else in1.at[k - 1]
        speed = out2.at[me_l] if k == 0 else in2.at[k - 1]
        for c in range(3):
            v = speed[c]
            moved_ref[3 + c, at, :] = v
            moved_ref[c, at, :] = place[c] + STEP * v

    for t in range(2):
        wait_halo_sent(t)
        for copy in grp_copies(t):
            copy.wait_send()
    for phase in range(3):
        for copy in a2a_copies(phase):
            copy.wait_send()


def per_device(nl, nh, nw, positions, velocities, radius, counts, cell_index, fluid_velocity, plan):
    gl, gh, gw, slots = radius.shape
    bins = gl * gh * gw
    cap = max(2, 2 * bins // nl)
    spread = fluid_velocity.shape[1] // 128
    groups = nh * nw
    dims = (gl, gh, gw, cap, spread)

    def count(n):
        return 1 if n <= 2 else 2

    sl, sh, sw = count(nl), count(nh), count(nw)
    halos = sl * gh * gw + sh * gl * gw + sw * gl * gh
    blocks = gl * (gh * gw + 2 * (gh - 1) * gw + 2 * gh * (gw - 1)) + 2 * (gl - 1) * gh * gw + halos
    vmem = pltpu.VMEM
    scratch = [
        vmem((bins, 8, 128), F32), vmem((bins, 8, 128), F32), vmem((bins, 8, 128), F32),
        vmem((bins, 8, 128), F32), vmem((bins, 8, 128), F32),
        vmem((2, gl, gh, gw, 8, 128), F32),
        vmem((2, sl, gh, gw, 8, 128), F32), vmem((2, sh, gl, gw, 8, 128), F32), vmem((2, sw, gl, gh, 8, 128), F32),
        vmem((bins + halos, 128, 64), BF16), vmem((bins, 64, 256), BF16), vmem((bins + halos, 128, 384), F32),
        vmem((bins, 32, 128), F32), vmem((blocks, 128, 128), F32),
        vmem((gl, 128, gh * gw * 128), BF16),
        vmem((groups, 8, 128), F32), vmem((groups, 8, 128), F32), vmem((max(1, groups - 1), 8, 128), F32),
        vmem((nl, 2, cap, 128), F32), vmem((nl, 3, cap, 128), F32), vmem((nl, 3, cap, 128), F32),
        vmem((nl - 1, 2, cap, 128), F32), vmem((nl - 1, 3, cap, 128), F32), vmem((nl - 1, 3, cap, 128), F32),
        pltpu.SemaphoreType.DMA((2, 3, 2)), pltpu.SemaphoreType.DMA((2, 3, 2)),
        pltpu.SemaphoreType.DMA((2, groups)), pltpu.SemaphoreType.DMA((2, groups)),
        pltpu.SemaphoreType.DMA((3, nl)), pltpu.SemaphoreType.DMA((3, nl)),
    ]
    in_vmem = pl.BlockSpec(memory_space=pltpu.VMEM)
    in_smem = pl.BlockSpec(memory_space=pltpu.SMEM)
    moved, fluid_next = pl.pallas_call(
        functools.partial(kernel, nl, nh, nw, dims),
        out_shape=(
            jax.ShapeDtypeStruct((8, nl * cap, slots), F32),
            jax.ShapeDtypeStruct(fluid_velocity.shape, F32),
        ),
        in_specs=[in_vmem, in_vmem, in_vmem, in_smem, in_vmem, in_vmem, in_vmem],
        out_specs=(in_vmem, in_vmem),
        scratch_shapes=scratch,
        compiler_params=pltpu.CompilerParams(
            collective_id=0, has_side_effects=True, vmem_limit_bytes=48 * 1024 * 1024
        ),
    )(positions, velocities, radius, counts, cell_index, fluid_velocity, plan.reshape(1, bins))
    return moved.reshape(8, 1, 1, nl * cap, slots), fluid_next


def solution(mesh):
    sizes = dict(mesh.shape)
    in_specs = (
        P(None, ("section", "len"), "ht", "wd", None),
        P(None, ("section", "len"), "ht", "wd", None),
        P(("section", "len"), "ht", "wd", None),
        P(("section", "len"), "ht", "wd"),
        P(("section", "len"), "ht", "wd", None),
        P(None, ("section", "len", "ht", "wd")),
        P(("section", "len"), "ht", "wd", None, None),
    )
    out_specs = (
        P(None, "ht", "wd", ("section", "len"), None),
        P(None, ("section", "len", "ht", "wd")),
    )
    body = functools.partial(per_device, sizes["len"], sizes["ht"], sizes["wd"])
    return jax.shard_map(body, mesh=mesh, in_specs=in_specs, out_specs=out_specs, check_vma=False)
```

```python
import functools

import jax
import jax.numpy as jnp
from jax import lax
from jax.experimental import pallas as pl
from jax.experimental.pallas import tpu as pltpu
from jax.sharding import PartitionSpec as P

STEP = 0.1
COUPLE = 0.5
RADIUS_REF = 0.45
PARK = 64.0
MESH = pl.DeviceIdType.MESH
F32 = jnp.float32
BF16 = jnp.bfloat16


def dot(a, b):
    return jnp.dot(a, b, preferred_element_type=F32)


def dot_t(a, b):
    return lax.dot_general(a, b, (((1,), (1,)), ((), ())), preferred_element_type=F32)


def split3(x):
    h = x.astype(BF16).astype(F32)
    rest = x - h
    m = rest.astype(BF16).astype(F32)
    return h, m, rest - m


def axis_sides(axis, n, size):
    me = lax.axis_index(axis)
    if n == 1:
        return []
    if n == 2:
        return [(1 - me, (size - 1) * (1 - me), size * (1 - me) - me, None)]
    return [(me - 1, 0, -1, me > 0), (me + 1, size - 1, size, me < n - 1)]


def maybe(cond, fn):
    if cond is None:
        fn()
    else:
        pl.when(cond)(fn)


def kernel(
    nl, nh, nw, dims,
    pos_hbm, vel_hbm, rad_hbm, cnt_hbm, cell_hbm, flu_hbm, plan_hbm,
    moved_ref, fnext_ref,
    pos_ref, vel_ref, rad_ref, cnt_ref, cell_ref, flu_ref, plan_ref, load_sem,
    xr, vr, ur, accr, lv, xp, hl, hh, hw, lt, rr, pc, gg, tc, oh, ft, pb, pr,
    out0, out1, out2, in0, in1, in2,
    halo_send, halo_recv, grp_send, grp_recv, a2a_send, a2a_recv,
):
    gl, gh, gw, cap, spread = dims
    bins = gl * gh * gw
    layer = gh * gw
    groups = nh * nw
    me_l = lax.axis_index("len")
    me_h = lax.axis_index("ht")
    me_w = lax.axis_index("wd")
    me_g = me_h * nw + me_w

    loads = []
    for k, (source, target) in enumerate((
        (pos_hbm, pos_ref), (vel_hbm, vel_ref), (rad_hbm, rad_ref), (cnt_hbm, cnt_ref),
        (cell_hbm, cell_ref), (flu_hbm, flu_ref), (plan_hbm, plan_ref),
    )):
        loads.append(pltpu.make_async_copy(source, target, load_sem.at[k]))
    for load in loads:
        load.start()

    barrier = pltpu.get_barrier_semaphore()

    def len_peer(k):
        return lax.rem(me_l + k, nl)

    def grp_peer(k):
        return lax.rem(me_g + k, groups)

    def grp_id(k):
        g = grp_peer(k)
        return {"ht": g // nw, "wd": lax.rem(g, nw)}

    for k in range(1, nl):
        pl.semaphore_signal(barrier, inc=1, device_id={"len": len_peer(k)}, device_id_type=MESH)
    for k in range(1, groups):
        pl.semaphore_signal(barrier, inc=1, device_id=grp_id(k), device_id_type=MESH)

    row = lax.broadcasted_iota(jnp.int32, (8, 128), 0)
    lane = lax.broadcasted_iota(jnp.int32, (1, 128), 1)
    layer_lane = lax.broadcasted_iota(jnp.int32, (1, gl), 1)

    for load in loads:
        load.wait()

    def load_layer(l, _):
        for h in range(gh):
            for w in range(gw):
                b = l * layer + h * gw + w
                xr[b] = jnp.zeros((8, 128), F32)
                vr[b] = jnp.zeros((8, 128), F32)
                for c in range(3):
                    xr[b, c : c + 1, :] = pos_ref[c, l, h, w : w + 1, :]
                    vr[b, c : c + 1, :] = vel_ref[c, l, h, w : w + 1, :]
                xr[b, 3:4, :] = rad_ref[l, h, w : w + 1, :]
                numbers = cnt_ref[h, w : w + 1, :].astype(F32)
                number = jnp.sum(jnp.where(layer_lane == l, numbers, 0.0), axis=1, keepdims=True)
                live = lane.astype(F32) < number
                lv[b] = jnp.broadcast_to(jnp.where(live, 1.0, 0.0), (8, 128))
                xp[0, l, h, w] = jnp.where((lv[b] > 0.5) | (row >= 3), xr[b], PARK)
        return 0

    lax.fori_loop(0, gl, load_layer, 0)
    for c in range(3):
        for s in range(spread):
            ft[0, c * spread + s : c * spread + s + 1, :] = flu_ref[c : c + 1, s * 128 : (s + 1) * 128]
    for r_ in range(3 * spread, 8):
        ft[0, r_ : r_ + 1, :] = jnp.zeros((1, 128), F32)

    plans = []
    for axis, n, size, ref in (("len", nl, gl, hl), ("ht", nh, gh, hh), ("wd", nw, gw, hw)):
        plans.append((axis, ref, axis_sides(axis, n, size)))
    empty = jnp.where(row < 3, PARK, RADIUS_REF)
    for axis, ref, sides in plans:
        for s, (partner, face, coord, exists) in enumerate(sides):
            if exists is not None:

                def fill(ref=ref, s=s):
                    for t in range(2):
                        ref[t, s] = jnp.broadcast_to(empty, ref.shape[2:])

                pl.when(jnp.logical_not(exists))(fill)

    pl.semaphore_wait(barrier, nl - 1 + groups - 1)

    def halo_copies(t):
        res = []
        for a, (axis, ref, sides) in enumerate(plans):
            for s, (partner, face, coord, exists) in enumerate(sides):
                back = s if len(sides) == 1 else 1 - s
                src = (xp.at[t, face], xp.at[t, :, face], xp.at[t, :, :, face])[a]
                send = pltpu.make_async_remote_copy(
                    src_ref=src, dst_ref=ref.at[t, back],
                    send_sem=halo_send.at[t, a, s], recv_sem=halo_recv.at[t, a, back],
                    device_id={axis: partner}, device_id_type=MESH,
                )
                recv = pltpu.make_async_remote_copy(
                    src_ref=src, dst_ref=ref.at[t, s],
                    send_sem=halo_send.at[t, a, s], recv_sem=halo_recv.at[t, a, s],
                    device_id={axis: partner}, device_id_type=MESH,
                )
                res.append((send, recv, exists))
        return res

    def start_halo(t):
        for send, recv, exists in halo_copies(t):
            maybe(exists, send.start)

    def wait_halo(t):
        for send, recv, exists in halo_copies(t):
            maybe(exists, recv.wait_recv)

    def wait_halo_sent(t):
        for send, recv, exists in halo_copies(t):
            maybe(exists, send.wait_send)

    def grp_copies(phase):
        res = []
        for k in range(1, groups):
            src = ft.at[0] if phase == 0 else pb.at[grp_peer(k)]
            dst = ft.at[k] if phase == 0 else pr.at[k - 1]
            res.append(pltpu.make_async_remote_copy(
                src_ref=src, dst_ref=dst, send_sem=grp_send.at[phase, k - 1],
                recv_sem=grp_recv.at[phase, k - 1], device_id=grp_id(k), device_id_type=MESH))
        return res

    def a2a_copies(phase):
        src, dst = ((out0, in0), (out1, in1), (out2, in2))[phase]
        res = []
        for k in range(1, nl):
            res.append(pltpu.make_async_remote_copy(
                src_ref=src.at[len_peer(k)], dst_ref=dst.at[k - 1], send_sem=a2a_send.at[phase, k - 1],
                recv_sem=a2a_recv.at[phase, k - 1], device_id={"len": len_peer(k)}, device_id_type=MESH))
        return res

    start_halo(0)
    for copy in grp_copies(0):
        copy.start()

    dest = plan_ref[...]
    marks = jnp.where(dest == lax.broadcasted_iota(jnp.int32, (16, bins), 0), 1.0, 0.0)
    before = jnp.where(
        lax.broadcasted_iota(jnp.int32, (bins, bins), 0) < lax.broadcasted_iota(jnp.int32, (bins, bins), 1),
        1.0, 0.0)
    earlier = dot(marks.astype(BF16), before.astype(BF16))
    rank = jnp.sum(earlier * marks, axis=0, keepdims=True)
    slot = dest * cap + rank.astype(jnp.int32)
    sel = jnp.where(slot == lax.broadcasted_iota(jnp.int32, (nl * cap, bins), 0), 1.0, 0.0)
    sel3 = jnp.concatenate([sel, sel, sel], axis=1).astype(BF16)

    def pack(values, out, c):
        parts = jnp.concatenate(split3(values), axis=0).astype(BF16)
        got = dot(sel3, parts)
        for d in range(nl):
            out[d, c] = got[d * cap : (d + 1) * cap]

    alive = lv[:, 0, :]
    pack(xr[:, 3, :] * alive, out0, 0)
    pack(alive, out0, 1)
    for copy in a2a_copies(0):
        copy.start()

    mid = ((gl - 1) / 2 + 0.5, gh / 2, gw / 2)

    def coords(tile, where):
        off = jnp.zeros((8, 128), F32)
        for c in range(3):
            off = jnp.where(row == c, jnp.asarray(where[c], F32) - mid[c], off)
        return jnp.where(row < 3, tile + off, 0.0)

    zero = jnp.zeros((8, 128), F32)
    part_row = lax.broadcasted_iota(jnp.int32, (32, 384), 0)
    part_comp = lax.broadcasted_iota(jnp.int32, (32, 384), 1) // 128
    spread_out = jnp.where((part_row == part_comp) | (part_row == part_comp + 16) | (part_row == part_comp + 27), 1.0, 0.0).astype(BF16)

    def rows_of(*values):
        out = zero
        for k, value in enumerate(values):
            if value is not None:
                out = jnp.where(row == k, value, out)
        return out

    def halves(place):
        return split3(place) + (split3(jnp.sum(place * place, axis=0, keepdims=True)),)

    def right_side(t, index, tile, place):
        h, m, l, (nh_, nm_, nl_) = halves(place)
        first = jnp.where(row < 3, 2.0 * h, rows_of(None, None, None, 1.0, nh_, None, None, 1.0))
        second = jnp.where(row < 3, 2.0 * m, jnp.where(row == 3, pltpu.roll(2.0 * l, 1, 0), rows_of(None, None, None, None, nm_)))
        third = jnp.where(row < 3, 2.0 * h, rows_of(None, None, None, 1.0, None, None, None, nl_))
        fourth = jnp.where(row < 3, 2.0 * m, jnp.where(row < 6, pltpu.roll(2.0 * h, 3, 0), pltpu.roll(2.0 * l, 6, 0)))
        rr[index, :, 0:128] = jnp.concatenate([first, second, third, fourth], axis=0).astype(BF16)
        if t == 0:
            rh, rm, _ = split3(tile[3:4])
            reach = [rows_of(None, None, None, None, None, 1.0, rh), rows_of(None, None, None, None, None, None, rm),
                     rows_of(None, None, None, None, None, 1.0), zero]
            rr[index, :, 128:256] = jnp.concatenate(reach, axis=0).astype(BF16)

    def left_side(index, tile, place):
        h, m, l, (nh_, nm_, nl_) = halves(place)
        rh, rm, _ = split3(tile[3:4])
        first = jnp.where(row < 3, h, rows_of(None, None, None, -nh_, -1.0, rh, 1.0, -nl_))
        third = jnp.where(row < 3, m, rows_of(None, None, None, -nm_, None, rm, None, -1.0))
        second = jnp.where(row == 3, pltpu.roll(h, 1, 0), first)
        fourth = jnp.where(row < 3, m, jnp.where(row < 6, pltpu.roll(l, 3, 0), pltpu.roll(h, 6, 0)))
        left = jnp.concatenate([first, second, third, fourth], axis=0).astype(BF16).T
        lt[index] = left
        pc[index] = dot(left, spread_out)

    def push(t, target, source, block):
        if t == 0:
            both = dot(lt[source], rr[target])
            dist = both[:, :128]
            inv = pl.reciprocal(both[:, 128:], approx=False)
            inv = inv * inv
            tc[block] = inv
        else:
            dist = dot(lt[source], rr[target, :, 0:128])
            inv = tc[block]
        e = jnp.exp(dist * inv)
        acc = [None] * 4
        for k in range(16):
            piece = e[8 * k : 8 * k + 8]
            terms = [piece * pc[source, 8 * k : 8 * k + 8, 128 * c : 128 * c + 128] for c in range(3)] + [piece]
            acc = terms if k == 0 else [a + b for a, b in zip(acc, terms)]
        return jnp.concatenate(acc, axis=0)

    near = []
    for h in range(gh):
        for w in range(gw):
            near.append((h * gw + w, h * gw + w))
            for h2, w2 in ((h - 1, w), (h + 1, w), (h, w - 1), (h, w + 1)):
                if 0 <= h2 < gh and 0 <= w2 < gw:
                    near.append((h * gw + w, h2 * gw + w2))
    per_layer = len(near)
    base_len = gl * per_layer
    base_halo = base_len + 2 * (gl - 1) * layer

    def prepare(t):
        def one(l, _):
            for h in range(gh):
                for w in range(gw):
                    b = l * layer + h * gw + w
                    tile = xp[t, l, h, w]
                    place = coords(tile, (l, h, w))
                    right_side(t, b, tile, place)
                    left_side(b, tile, place)
            return 0

        lax.fori_loop(0, gl, one, 0)

    def interior(t):
        def one(l, _):
            base = l * layer
            sums = [None] * layer
            for n_, (i, j) in enumerate(near):
                got = push(t, base + i, base + j, l * per_layer + n_)
                sums[i] = got if sums[i] is None else sums[i] + got
            for n_ in range(layer):
                gg[base + n_] = sums[n_]
            return 0

        lax.fori_loop(0, gl, one, 0)

        def along(l, _):
            base = l * layer
            ups, downs = [], []
            for n_ in range(layer):
                block = base_len + 2 * (base + n_)
                ups.append(push(t, base + layer + n_, base + n_, block))
                downs.append(push(t, base + n_, base + layer + n_, block + 1))
            for n_ in range(layer):
                gg[base + n_] += downs[n_]
                gg[base + layer + n_] += ups[n_]
            return 0

        lax.fori_loop(0, gl - 1, along, 0)

    def boundary(t):
        at = bins
        for s, (partner, face, coord, exists) in enumerate(plans[0][2]):
            sums = []
            for h in range(gh):
                for w in range(gw):
                    tile = hl[t, s, h, w]
                    left_side(at + h * gw + w, tile, coords(tile, (coord, h, w)))
            for n_ in range(layer):
                sums.append(push(t, face * layer + n_, at + n_, base_halo + at - bins + n_))
            for n_ in range(layer):
                gg[face * layer + n_] += sums[n_]
            at += layer
        for a, across in ((1, gw), (2, gh)):
            ref = plans[a][1]
            for s, (partner, face, coord, exists) in enumerate(plans[a][2]):
                step = 2 if gl % 2 == 0 else 1

                def one(p, _, ref=ref, s=s, face=face, coord=coord, a=a, across=across, at=at, step=step):
                    targets, sums = [], []
                    for q in range(step):
                        l = p * step + q
                        for y in range(across):
                            tile = ref[t, s, l, y]
                            place = coords(tile, (l, coord, y) if a == 1 else (l, y, coord))
                            left_side(at + l * across + y, tile, place)
                    for q in range(step):
                        l = p * step + q
                        for y in range(across):
                            n_ = at + l * across + y
                            target = l * layer + (face * gw + y if a == 1 else y * gw + face)
                            targets.append(target)
                            sums.append(push(t, target, n_, base_halo + n_ - bins))
                    for target, got in zip(targets, sums):
                        gg[target] += got
                    return 0

                lax.fori_loop(0, gl // step, one, 0)
                at += gl * across

    lo_rows = lax.broadcasted_iota(jnp.int32, (128, 128), 0)

    def hi_mask(cells, g):
        return lax.shift_right_logical(cells, 7) == g * spread + lax.rem(row, spread)

    def read_fluid():
        for copy in grp_copies(0):
            copy.wait_recv()
        table = []
        for k in range(groups):
            table.append(ft[k])
        table = jnp.concatenate(table, axis=0)
        table = jnp.concatenate(split3(table), axis=0).astype(BF16)

        def one(l, _):
            for h in range(gh):
                for w in range(gw):
                    n_ = h * gw + w
                    cells = cell_ref[l, h, w : w + 1, :]
                    low = lax.rem(cells, 128)
                    oh[l, :, n_ * 128 : (n_ + 1) * 128] = jnp.where(low == lo_rows, 1.0, 0.0).astype(BF16)
            got = dot(table, oh[l])
            full = got[: groups * 8] + got[groups * 8 : groups * 16] + got[groups * 16 :]
            for h in range(gh):
                for w in range(gw):
                    n_ = h * gw + w
                    cells = cell_ref[l, h, w : w + 1, :]
                    mine = full[:, n_ * 128 : (n_ + 1) * 128]
                    u = jnp.zeros((8, 128), F32)
                    for k in range(groups):
                        g = lax.rem(me_g - k + groups, groups)
                        u = u + jnp.where(hi_mask(cells, g), mine[k * 8 : (k + 1) * 8], 0.0)
                    b = l * layer + n_
                    ur[b] = jnp.zeros((8, 128), F32)
                    for c in range(3):
                        ur[b, c : c + 1, :] = jnp.sum(u[c * spread : (c + 1) * spread], axis=0, keepdims=True)
            return 0

        lax.fori_loop(0, gl, one, 0)

    def update(t):
        def one(l, _):
            for h in range(gh):
                for w in range(gw):
                    b = l * layer + h * gw + w
                    tile = xr[b]
                    radius = tile[3:4]
                    ratio = radius * (1.0 / RADIUS_REF)
                    mass = ratio * ratio * ratio
                    place = coords(xp[t, l, h, w], (l, h, w))
                    g = gg[b]
                    rows = [jnp.sum(g[8 * c : 8 * c + 8], axis=0, keepdims=True) for c in range(4)]
                    total = jnp.concatenate(rows + rows, axis=0)
                    force = place * rows[3] - total
                    speed = vr[b]
                    drag = radius * (ur[b] - speed)
                    accr[b] = drag if t == 0 else accr[b] + drag
                    speed = speed + STEP * (force + drag) * (1.0 / mass)
                    alive = lv[b] > 0.5
                    speed = jnp.where((row < 3) & alive, speed, 0.0)
                    vr[b] = speed
                    if t == 0:
                        tile = tile + STEP * speed
                        xr[b] = tile
                        xp[1, l, h, w] = jnp.where(alive | (row >= 3), tile, PARK)
            return 0

        lax.fori_loop(0, gl, one, 0)

    prepare(0)
    interior(0)
    read_fluid()
    wait_halo(0)
    boundary(0)
    update(0)
    start_halo(1)
    for c in range(3):
        pack(xr[:, c, :] * alive, out1, c)
    for copy in a2a_copies(1):
        copy.start()

    prepare(1)
    interior(1)
    wait_halo(1)
    boundary(1)
    update(1)
    for c in range(3):
        pack(vr[:, c, :], out2, c)
    for copy in a2a_copies(2):
        copy.start()

    def cell_sums(l, total):
        lefts = []
        for h in range(gh):
            for w in range(gw):
                b = l * layer + h * gw + w
                cells = cell_ref[l, h, w : w + 1, :]
                radius = xr[b, 3:4, :]
                ratio = radius * (1.0 / RADIUS_REF)
                live_row = lv[b, 0:1, :]
                rows = [accr[b, c : c + 1, :] * live_row for c in range(3)] + [ratio * ratio * ratio * live_row]
                term = jnp.concatenate([rows[r_ // spread] for r_ in range(4 * spread)], axis=0)
                parts = split3(term)
                pieces = []
                for part in parts:
                    for g in range(groups):
                        pieces.append(jnp.where(hi_mask(cells, g), part, 0.0))
                lefts.append(jnp.concatenate(pieces, axis=0).astype(BF16))
        return total + dot_t(jnp.concatenate(lefts, axis=1), oh[l])

    sums = lax.fori_loop(0, gl, cell_sums, jnp.zeros((groups * 24, 128), F32))
    sums = sums[: groups * 8] + sums[groups * 8 : groups * 16] + sums[groups * 16 :]
    for g in range(groups):
        pb[g] = sums[g * 8 : (g + 1) * 8]
    for copy in grp_copies(1):
        copy.start()

    def landed(own, arrived, c, put):
        put(me_l, own[me_l, c])
        for k in range(1, nl):
            put(lax.rem(me_l - k + nl, nl), arrived[k - 1, c])

    for copy in a2a_copies(0) + a2a_copies(1):
        copy.wait_recv()
    for k in range(nl):
        source = lax.rem(me_l - k + nl, nl)
        at = pl.ds(source * cap, cap)
        early = out0.at[me_l] if k == 0 else in0.at[k - 1]
        for c in range(2):
            moved_ref[6 + c, at, :] = early[c]

    for copy in grp_copies(1):
        copy.wait_recv()
    whole = pb[me_g]
    for k in range(groups - 1):
        whole = whole + pr[k]
    mass_rows = whole[3 * spread : 4 * spread]
    for c in range(3):
        ratio = whole[c * spread : (c + 1) * spread] / (1.0 + mass_rows)
        fresh = ft[0, c * spread : (c + 1) * spread, :] - COUPLE * ratio
        for s in range(spread):
            fnext_ref[c : c + 1, s * 128 : (s + 1) * 128] = fresh[s : s + 1]

    for copy in a2a_copies(2):
        copy.wait_recv()
    for k in range(nl):
        source = lax.rem(me_l - k + nl, nl)
        at = pl.ds(source * cap, cap)
        place = out1.at[me_l] if k == 0 else in1.at[k - 1]
        speed = out2.at[me_l] if k == 0 else in2.at[k - 1]
        for c in range(3):
            v = speed[c]
            moved_ref[3 + c, at, :] = v
            moved_ref[c, at, :] = place[c] + STEP * v

    for t in range(2):
        wait_halo_sent(t)
        for copy in grp_copies(t):
            copy.wait_send()
    for phase in range(3):
        for copy in a2a_copies(phase):
            copy.wait_send()


def per_device(nl, nh, nw, positions, velocities, radius, counts, cell_index, fluid_velocity, plan):
    gl, gh, gw, slots = radius.shape
    bins = gl * gh * gw
    cap = max(2, 2 * bins // nl)
    spread = fluid_velocity.shape[1] // 128
    groups = nh * nw
    dims = (gl, gh, gw, cap, spread)

    def count(n):
        return 1 if n <= 2 else 2

    sl, sh, sw = count(nl), count(nh), count(nw)
    halos = sl * gh * gw + sh * gl * gw + sw * gl * gh
    blocks = gl * (gh * gw + 2 * (gh - 1) * gw + 2 * gh * (gw - 1)) + 2 * (gl - 1) * gh * gw + halos
    vmem = pltpu.VMEM
    scratch = [
        vmem(positions.shape, F32), vmem(velocities.shape, F32), vmem(radius.shape, F32), vmem((gh, gw, gl), jnp.int32),
        vmem(cell_index.shape, jnp.int32), vmem(fluid_velocity.shape, F32), vmem((1, bins), jnp.int32),
        pltpu.SemaphoreType.DMA((7,)),
        vmem((bins, 8, 128), F32), vmem((bins, 8, 128), F32), vmem((bins, 8, 128), F32),
        vmem((bins, 8, 128), F32), vmem((bins, 8, 128), F32),
        vmem((2, gl, gh, gw, 8, 128), F32),
        vmem((2, sl, gh, gw, 8, 128), F32), vmem((2, sh, gl, gw, 8, 128), F32), vmem((2, sw, gl, gh, 8, 128), F32),
        vmem((bins + halos, 128, 32), BF16), vmem((bins, 32, 256), BF16), vmem((bins + halos, 128, 384), F32),
        vmem((bins, 32, 128), F32), vmem((blocks, 128, 128), F32),
        vmem((gl, 128, gh * gw * 128), BF16),
        vmem((groups, 8, 128), F32), vmem((groups, 8, 128), F32), vmem((max(1, groups - 1), 8, 128), F32),
        vmem((nl, 2, cap, 128), F32), vmem((nl, 3, cap, 128), F32), vmem((nl, 3, cap, 128), F32),
        vmem((nl - 1, 2, cap, 128), F32), vmem((nl - 1, 3, cap, 128), F32), vmem((nl - 1, 3, cap, 128), F32),
        pltpu.SemaphoreType.DMA((2, 3, 2)), pltpu.SemaphoreType.DMA((2, 3, 2)),
        pltpu.SemaphoreType.DMA((2, groups)), pltpu.SemaphoreType.DMA((2, groups)),
        pltpu.SemaphoreType.DMA((3, nl)), pltpu.SemaphoreType.DMA((3, nl)),
    ]
    in_vmem = pl.BlockSpec(memory_space=pltpu.VMEM)
    anywhere = pl.BlockSpec(memory_space=pl.ANY)
    moved, fluid_next = pl.pallas_call(
        functools.partial(kernel, nl, nh, nw, dims),
        out_shape=(
            jax.ShapeDtypeStruct((8, nl * cap, slots), F32),
            jax.ShapeDtypeStruct(fluid_velocity.shape, F32),
        ),
        in_specs=[anywhere] * 7,
        out_specs=(in_vmem, in_vmem),
        scratch_shapes=scratch,
        compiler_params=pltpu.CompilerParams(
            collective_id=0, has_side_effects=True, vmem_limit_bytes=56 * 1024 * 1024
        ),
    )(positions, velocities, radius, counts.transpose(1, 2, 0), cell_index, fluid_velocity, plan.reshape(1, bins))
    return moved.reshape(8, 1, 1, nl * cap, slots), fluid_next


def solution(mesh):
    sizes = dict(mesh.shape)
    in_specs = (
        P(None, ("section", "len"), "ht", "wd", None),
        P(None, ("section", "len"), "ht", "wd", None),
        P(("section", "len"), "ht", "wd", None),
        P(("section", "len"), "ht", "wd"),
        P(("section", "len"), "ht", "wd", None),
        P(None, ("section", "len", "ht", "wd")),
        P(("section", "len"), "ht", "wd", None, None),
    )
    out_specs = (
        P(None, "ht", "wd", ("section", "len"), None),
        P(None, ("section", "len", "ht", "wd")),
    )
    body = functools.partial(per_device, sizes["len"], sizes["ht"], sizes["wd"])
    return jax.shard_map(body, mesh=mesh, in_specs=in_specs, out_specs=out_specs, check_vma=False)
```

```python
import functools

import jax
import jax.numpy as jnp
from jax import lax
from jax.experimental import pallas as pl
from jax.experimental.pallas import tpu as pltpu
from jax.sharding import PartitionSpec as P

STEP = 0.1
COUPLE = 0.5
RADIUS_REF = 0.45
PARK = 64.0
MESH = pl.DeviceIdType.MESH
F32 = jnp.float32
BF16 = jnp.bfloat16


def dot(a, b):
    return jnp.dot(a, b, preferred_element_type=F32)


def dot_t(a, b):
    return lax.dot_general(a, b, (((1,), (1,)), ((), ())), preferred_element_type=F32)


def split3(x):
    h = x.astype(BF16).astype(F32)
    rest = x - h
    m = rest.astype(BF16).astype(F32)
    return h, m, rest - m


def axis_sides(axis, n, size):
    me = lax.axis_index(axis)
    if n == 1:
        return []
    if n == 2:
        return [(1 - me, (size - 1) * (1 - me), size * (1 - me) - me, None)]
    return [(me - 1, 0, -1, me > 0), (me + 1, size - 1, size, me < n - 1)]


def maybe(cond, fn):
    if cond is None:
        fn()
    else:
        pl.when(cond)(fn)


def kernel(
    nl, nh, nw, dims,
    pos_hbm, vel_hbm, rad_hbm, cnt_hbm, cell_hbm, flu_hbm, plan_hbm,
    moved_ref, fnext_ref,
    pos_ref, vel_ref, rad_ref, cnt_ref, cell_ref, flu_ref, plan_ref, load_sem,
    xr, vr, ur, accr, lv, xp, hl, hh, hw, lt, rr, pc, gg, tc, oh, ft, pb, pr,
    out0, out1, out2, in0, in1, in2,
    halo_send, halo_recv, grp_send, grp_recv, a2a_send, a2a_recv,
):
    gl, gh, gw, cap, spread = dims
    bins = gl * gh * gw
    layer = gh * gw
    groups = nh * nw
    me_l = lax.axis_index("len")
    me_h = lax.axis_index("ht")
    me_w = lax.axis_index("wd")
    me_g = me_h * nw + me_w

    loads = []
    for k, (source, target) in enumerate((
        (pos_hbm, pos_ref), (vel_hbm, vel_ref), (rad_hbm, rad_ref), (cnt_hbm, cnt_ref),
        (cell_hbm, cell_ref), (flu_hbm, flu_ref), (plan_hbm, plan_ref),
    )):
        loads.append(pltpu.make_async_copy(source, target, load_sem.at[k]))
    for load in loads:
        load.start()

    barrier = pltpu.get_barrier_semaphore()

    def len_peer(k):
        return lax.rem(me_l + k, nl)

    def grp_peer(k):
        return lax.rem(me_g + k, groups)

    def grp_id(k):
        g = grp_peer(k)
        return {"ht": g // nw, "wd": lax.rem(g, nw)}

    for k in range(1, nl):
        pl.semaphore_signal(barrier, inc=1, device_id={"len": len_peer(k)}, device_id_type=MESH)
    for k in range(1, groups):
        pl.semaphore_signal(barrier, inc=1, device_id=grp_id(k), device_id_type=MESH)

    row = lax.broadcasted_iota(jnp.int32, (8, 128), 0)
    lane = lax.broadcasted_iota(jnp.int32, (1, 128), 1)
    layer_lane = lax.broadcasted_iota(jnp.int32, (1, gl), 1)

    for load in loads:
        load.wait()

    def load_layer(l, _):
        for h in range(gh):
            for w in range(gw):
                b = l * layer + h * gw + w
                xr[b] = jnp.zeros((8, 128), F32)
                vr[b] = jnp.zeros((8, 128), F32)
                for c in range(3):
                    xr[b, c : c + 1, :] = pos_ref[c, l, h, w : w + 1, :]
                    vr[b, c : c + 1, :] = vel_ref[c, l, h, w : w + 1, :]
                xr[b, 3:4, :] = rad_ref[l, h, w : w + 1, :]
                numbers = cnt_ref[h, w : w + 1, :].astype(F32)
                number = jnp.sum(jnp.where(layer_lane == l, numbers, 0.0), axis=1, keepdims=True)
                live = lane.astype(F32) < number
                lv[b] = jnp.broadcast_to(jnp.where(live, 1.0, 0.0), (8, 128))
                xp[0, l, h, w] = jnp.where((lv[b] > 0.5) | (row >= 3), xr[b], PARK)
        return 0

    lax.fori_loop(0, gl, load_layer, 0)
    for c in range(3):
        for s in range(spread):
            ft[0, c * spread + s : c * spread + s + 1, :] = flu_ref[c : c + 1, s * 128 : (s + 1) * 128]
    for r_ in range(3 * spread, 8):
        ft[0, r_ : r_ + 1, :] = jnp.zeros((1, 128), F32)

    plans = []
    for axis, n, size, ref in (("len", nl, gl, hl), ("ht", nh, gh, hh), ("wd", nw, gw, hw)):
        plans.append((axis, ref, axis_sides(axis, n, size)))
    empty = jnp.where(row < 3, PARK, RADIUS_REF)
    for axis, ref, sides in plans:
        for s, (partner, face, coord, exists) in enumerate(sides):
            if exists is not None:

                def fill(ref=ref, s=s):
                    for t in range(2):
                        ref[t, s] = jnp.broadcast_to(empty, ref.shape[2:])

                pl.when(jnp.logical_not(exists))(fill)

    pl.semaphore_wait(barrier, nl - 1 + groups - 1)

    def halo_copies(t):
        res = []
        for a, (axis, ref, sides) in enumerate(plans):
            for s, (partner, face, coord, exists) in enumerate(sides):
                back = s if len(sides) == 1 else 1 - s
                src = (xp.at[t, face], xp.at[t, :, face], xp.at[t, :, :, face])[a]
                send = pltpu.make_async_remote_copy(
                    src_ref=src, dst_ref=ref.at[t, back],
                    send_sem=halo_send.at[t, a, s], recv_sem=halo_recv.at[t, a, back],
                    device_id={axis: partner}, device_id_type=MESH,
                )
                recv = pltpu.make_async_remote_copy(
                    src_ref=src, dst_ref=ref.at[t, s],
                    send_sem=halo_send.at[t, a, s], recv_sem=halo_recv.at[t, a, s],
                    device_id={axis: partner}, device_id_type=MESH,
                )
                res.append((send, recv, exists))
        return res

    def start_halo(t):
        for send, recv, exists in halo_copies(t):
            maybe(exists, send.start)

    def wait_halo(t):
        for send, recv, exists in halo_copies(t):
            maybe(exists, recv.wait_recv)

    def wait_halo_sent(t):
        for send, recv, exists in halo_copies(t):
            maybe(exists, send.wait_send)

    def grp_copies(phase):
        res = []
        for k in range(1, groups):
            src = ft.at[0] if phase == 0 else pb.at[grp_peer(k)]
            dst = ft.at[k] if phase == 0 else pr.at[k - 1]
            res.append(pltpu.make_async_remote_copy(
                src_ref=src, dst_ref=dst, send_sem=grp_send.at[phase, k - 1],
                recv_sem=grp_recv.at[phase, k - 1], device_id=grp_id(k), device_id_type=MESH))
        return res

    def a2a_copies(phase):
        src, dst = ((out0, in0), (out1, in1), (out2, in2))[phase]
        res = []
        for k in range(1, nl):
            res.append(pltpu.make_async_remote_copy(
                src_ref=src.at[len_peer(k)], dst_ref=dst.at[k - 1], send_sem=a2a_send.at[phase, k - 1],
                recv_sem=a2a_recv.at[phase, k - 1], device_id={"len": len_peer(k)}, device_id_type=MESH))
        return res

    start_halo(0)
    for copy in grp_copies(0):
        copy.start()

    dest = plan_ref[...]
    marks = jnp.where(dest == lax.broadcasted_iota(jnp.int32, (16, bins), 0), 1.0, 0.0)
    before = jnp.where(
        lax.broadcasted_iota(jnp.int32, (bins, bins), 0) < lax.broadcasted_iota(jnp.int32, (bins, bins), 1),
        1.0, 0.0)
    earlier = dot(marks.astype(BF16), before.astype(BF16))
    rank = jnp.sum(earlier * marks, axis=0, keepdims=True)
    slot = dest * cap + rank.astype(jnp.int32)
    sel = jnp.where(slot == lax.broadcasted_iota(jnp.int32, (nl * cap, bins), 0), 1.0, 0.0)
    sel3 = jnp.concatenate([sel, sel, sel], axis=1).astype(BF16)

    def pack(values, out, c):
        parts = jnp.concatenate(split3(values), axis=0).astype(BF16)
        got = dot(sel3, parts)
        for d in range(nl):
            out[d, c] = got[d * cap : (d + 1) * cap]

    alive = lv[:, 0, :]
    pack(xr[:, 3, :] * alive, out0, 0)
    pack(alive, out0, 1)
    for copy in a2a_copies(0):
        copy.start()

    mid = ((gl - 1) / 2 + 0.5, gh / 2, gw / 2)

    def coords(tile, where):
        off = jnp.zeros((8, 128), F32)
        for c in range(3):
            off = jnp.where(row == c, jnp.asarray(where[c], F32) - mid[c], off)
        return jnp.where(row < 3, tile + off, 0.0)

    zero = jnp.zeros((8, 128), F32)
    part_row = lax.broadcasted_iota(jnp.int32, (32, 384), 0)
    part_comp = lax.broadcasted_iota(jnp.int32, (32, 384), 1) // 128
    spread_out = jnp.where((part_row == part_comp) | (part_row == part_comp + 16) | (part_row == part_comp + 27), 1.0, 0.0).astype(BF16)

    def rows_of(*values):
        out = zero
        for k, value in enumerate(values):
            if value is not None:
                out = jnp.where(row == k, value, out)
        return out

    def halves(place):
        return split3(place) + (split3(jnp.sum(place * place, axis=0, keepdims=True)),)

    def right_side(t, index, tile, place):
        h, m, l, (nh_, nm_, nl_) = halves(place)
        first = jnp.where(row < 3, 2.0 * h, rows_of(None, None, None, 1.0, nh_, None, None, 1.0))
        second = jnp.where(row < 3, 2.0 * m, jnp.where(row == 3, pltpu.roll(2.0 * l, 1, 0), rows_of(None, None, None, None, nm_)))
        third = jnp.where(row < 3, 2.0 * h, rows_of(None, None, None, 1.0, None, None, None, nl_))
        fourth = jnp.where(row < 3, 2.0 * m, jnp.where(row < 6, pltpu.roll(2.0 * h, 3, 0), pltpu.roll(2.0 * l, 6, 0)))
        rr[index, :, 0:128] = jnp.concatenate([first, second, third, fourth], axis=0).astype(BF16)
        if t == 0:
            rh, rm, _ = split3(tile[3:4])
            reach = [rows_of(None, None, None, None, None, 1.0, rh), rows_of(None, None, None, None, None, None, rm),
                     rows_of(None, None, None, None, None, 1.0), zero]
            rr[index, :, 128:256] = jnp.concatenate(reach, axis=0).astype(BF16)

    def left_side(tile, place):
        h, m, l, (nh_, nm_, nl_) = halves(place)
        rh, rm, _ = split3(tile[3:4])
        first = jnp.where(row < 3, h, rows_of(None, None, None, -nh_, -1.0, rh, 1.0, -nl_))
        third = jnp.where(row < 3, m, rows_of(None, None, None, -nm_, None, rm, None, -1.0))
        second = jnp.where(row == 3, pltpu.roll(h, 1, 0), first)
        fourth = jnp.where(row < 3, m, jnp.where(row < 6, pltpu.roll(l, 3, 0), pltpu.roll(h, 6, 0)))
        left = jnp.concatenate([first, second, third, fourth], axis=0).astype(BF16).T
        return left, dot(left, spread_out)

    def push(t, target, source, columns, block):
        if t == 0:
            both = dot(source, rr[target])
            dist = both[:, :128]
            inv = pl.reciprocal(both[:, 128:], approx=False)
            inv = inv * inv
            tc[block] = inv
        else:
            dist = dot(source, rr[target, :, 0:128])
            inv = tc[block]
        e = jnp.exp(dist * inv)
        acc = [None] * 4
        for k in range(16):
            piece = e[8 * k : 8 * k + 8]
            terms = [piece * columns[8 * k : 8 * k + 8, 128 * c : 128 * c + 128] for c in range(3)] + [piece]
            acc = terms if k == 0 else [a + b for a, b in zip(acc, terms)]
        return jnp.concatenate(acc, axis=0)

    near = []
    for h in range(gh):
        for w in range(gw):
            near.append((h * gw + w, h * gw + w))
            for h2, w2 in ((h - 1, w), (h + 1, w), (h, w - 1), (h, w + 1)):
                if 0 <= h2 < gh and 0 <= w2 < gw:
                    near.append((h * gw + w, h2 * gw + w2))
    per_layer = len(near)
    base_len = gl * per_layer
    base_halo = base_len + 2 * (gl - 1) * layer

    def prepare(t):
        def one(l, _):
            for h in range(gh):
                for w in range(gw):
                    b = l * layer + h * gw + w
                    tile = xp[t, l, h, w]
                    place = coords(tile, (l, h, w))
                    right_side(t, b, tile, place)
                    lt[b], pc[b] = left_side(tile, place)
            return 0

        lax.fori_loop(0, gl, one, 0)

    def interior(t):
        def one(l, _):
            base = l * layer
            sums = [None] * layer
            for n_, (i, j) in enumerate(near):
                got = push(t, base + i, lt[base + j], pc.at[base + j], l * per_layer + n_)
                sums[i] = got if sums[i] is None else sums[i] + got
            for n_ in range(layer):
                gg[base + n_] = sums[n_]
            return 0

        lax.fori_loop(0, gl, one, 0)

        def along(l, _):
            base = l * layer
            ups, downs = [], []
            for n_ in range(layer):
                block = base_len + 2 * (base + n_)
                ups.append(push(t, base + layer + n_, lt[base + n_], pc.at[base + n_], block))
                downs.append(push(t, base + n_, lt[base + layer + n_], pc.at[base + layer + n_], block + 1))
            for n_ in range(layer):
                gg[base + n_] += downs[n_]
                gg[base + layer + n_] += ups[n_]
            return 0

        lax.fori_loop(0, gl - 1, along, 0)

    def boundary(t):
        at = bins
        for s, (partner, face, coord, exists) in enumerate(plans[0][2]):
            sums = []
            for h in range(gh):
                for w in range(gw):
                    tile = hl[t, s, h, w]
                    source, columns = left_side(tile, coords(tile, (coord, h, w)))
                    n_ = h * gw + w
                    sums.append(push(t, face * layer + n_, source, columns, base_halo + at - bins + n_))
            for n_ in range(layer):
                gg[face * layer + n_] += sums[n_]
            at += layer
        for a, across in ((1, gw), (2, gh)):
            ref = plans[a][1]
            for s, (partner, face, coord, exists) in enumerate(plans[a][2]):
                step = 2 if gl % 2 == 0 else 1

                def one(p, _, ref=ref, s=s, face=face, coord=coord, a=a, across=across, at=at, step=step):
                    targets, sums = [], []
                    for q in range(step):
                        l = p * step + q
                        for y in range(across):
                            tile = ref[t, s, l, y]
                            place = coords(tile, (l, coord, y) if a == 1 else (l, y, coord))
                            source, columns = left_side(tile, place)
                            n_ = at + l * across + y
                            target = l * layer + (face * gw + y if a == 1 else y * gw + face)
                            targets.append(target)
                            sums.append(push(t, target, source, columns, base_halo + n_ - bins))
                    for target, got in zip(targets, sums):
                        gg[target] += got
                    return 0

                lax.fori_loop(0, gl // step, one, 0)
                at += gl * across

    lo_rows = lax.broadcasted_iota(jnp.int32, (128, 128), 0)

    def hi_mask(cells, g):
        return lax.shift_right_logical(cells, 7) == g * spread + lax.rem(row, spread)

    def read_fluid():
        for copy in grp_copies(0):
            copy.wait_recv()
        table = []
        for k in range(groups):
            table.append(ft[k])
        table = jnp.concatenate(table, axis=0)
        table = jnp.concatenate(split3(table), axis=0).astype(BF16)

        def one(l, _):
            for h in range(gh):
                for w in range(gw):
                    n_ = h * gw + w
                    cells = cell_ref[l, h, w : w + 1, :]
                    low = lax.rem(cells, 128)
                    oh[l, :, n_ * 128 : (n_ + 1) * 128] = jnp.where(low == lo_rows, 1.0, 0.0).astype(BF16)
            got = dot(table, oh[l])
            full = got[: groups * 8] + got[groups * 8 : groups * 16] + got[groups * 16 :]
            for h in range(gh):
                for w in range(gw):
                    n_ = h * gw + w
                    cells = cell_ref[l, h, w : w + 1, :]
                    mine = full[:, n_ * 128 : (n_ + 1) * 128]
                    u = jnp.zeros((8, 128), F32)
                    for k in range(groups):
                        g = lax.rem(me_g - k + groups, groups)
                        u = u + jnp.where(hi_mask(cells, g), mine[k * 8 : (k + 1) * 8], 0.0)
                    b = l * layer + n_
                    ur[b] = jnp.zeros((8, 128), F32)
                    for c in range(3):
                        ur[b, c : c + 1, :] = jnp.sum(u[c * spread : (c + 1) * spread], axis=0, keepdims=True)
            return 0

        lax.fori_loop(0, gl, one, 0)

    def update(t):
        def one(l, _):
            for h in range(gh):
                for w in range(gw):
                    b = l * layer + h * gw + w
                    tile = xr[b]
                    radius = tile[3:4]
                    ratio = radius * (1.0 / RADIUS_REF)
                    mass = ratio * ratio * ratio
                    place = coords(xp[t, l, h, w], (l, h, w))
                    g = gg[b]
                    rows = [jnp.sum(g[8 * c : 8 * c + 8], axis=0, keepdims=True) for c in range(4)]
                    total = jnp.concatenate(rows + rows, axis=0)
                    force = place * rows[3] - total
                    speed = vr[b]
                    drag = radius * (ur[b] - speed)
                    accr[b] = drag if t == 0 else accr[b] + drag
                    speed = speed + STEP * (force + drag) * (1.0 / mass)
                    alive = lv[b] > 0.5
                    speed = jnp.where((row < 3) & alive, speed, 0.0)
                    vr[b] = speed
                    if t == 0:
                        tile = tile + STEP * speed
                        xr[b] = tile
                        xp[1, l, h, w] = jnp.where(alive | (row >= 3), tile, PARK)
            return 0

        lax.fori_loop(0, gl, one, 0)

    prepare(0)
    interior(0)
    read_fluid()
    wait_halo(0)
    boundary(0)
    update(0)
    start_halo(1)
    for c in range(3):
        pack(xr[:, c, :] * alive, out1, c)
    for copy in a2a_copies(1):
        copy.start()

    prepare(1)
    interior(1)
    wait_halo(1)
    boundary(1)
    update(1)
    for c in range(3):
        pack(vr[:, c, :], out2, c)
    for copy in a2a_copies(2):
        copy.start()

    def cell_sums(l, total):
        lefts = []
        for h in range(gh):
            for w in range(gw):
                b = l * layer + h * gw + w
                cells = cell_ref[l, h, w : w + 1, :]
                radius = xr[b, 3:4, :]
                ratio = radius * (1.0 / RADIUS_REF)
                live_row = lv[b, 0:1, :]
                rows = [accr[b, c : c + 1, :] * live_row for c in range(3)] + [ratio * ratio * ratio * live_row]
                term = jnp.concatenate([rows[r_ // spread] for r_ in range(4 * spread)], axis=0)
                parts = split3(term)
                pieces = []
                for part in parts:
                    for g in range(groups):
                        pieces.append(jnp.where(hi_mask(cells, g), part, 0.0))
                lefts.append(jnp.concatenate(pieces, axis=0).astype(BF16))
        return total + dot_t(jnp.concatenate(lefts, axis=1), oh[l])

    sums = lax.fori_loop(0, gl, cell_sums, jnp.zeros((groups * 24, 128), F32))
    sums = sums[: groups * 8] + sums[groups * 8 : groups * 16] + sums[groups * 16 :]
    for g in range(groups):
        pb[g] = sums[g * 8 : (g + 1) * 8]
    for copy in grp_copies(1):
        copy.start()

    def landed(own, arrived, c, put):
        put(me_l, own[me_l, c])
        for k in range(1, nl):
            put(lax.rem(me_l - k + nl, nl), arrived[k - 1, c])

    for copy in a2a_copies(0) + a2a_copies(1):
        copy.wait_recv()
    for k in range(nl):
        source = lax.rem(me_l - k + nl, nl)
        at = pl.ds(source * cap, cap)
        early = out0.at[me_l] if k == 0 else in0.at[k - 1]
        for c in range(2):
            moved_ref[6 + c, at, :] = early[c]

    for copy in grp_copies(1):
        copy.wait_recv()
    whole = pb[me_g]
    for k in range(groups - 1):
        whole = whole + pr[k]
    mass_rows = whole[3 * spread : 4 * spread]
    for c in range(3):
        ratio = whole[c * spread : (c + 1) * spread] / (1.0 + mass_rows)
        fresh = ft[0, c * spread : (c + 1) * spread, :] - COUPLE * ratio
        for s in range(spread):
            fnext_ref[c : c + 1, s * 128 : (s + 1) * 128] = fresh[s : s + 1]

    for copy in a2a_copies(2):
        copy.wait_recv()
    for k in range(nl):
        source = lax.rem(me_l - k + nl, nl)
        at = pl.ds(source * cap, cap)
        place = out1.at[me_l] if k == 0 else in1.at[k - 1]
        speed = out2.at[me_l] if k == 0 else in2.at[k - 1]
        for c in range(3):
            v = speed[c]
            moved_ref[3 + c, at, :] = v
            moved_ref[c, at, :] = place[c] + STEP * v

    for t in range(2):
        wait_halo_sent(t)
        for copy in grp_copies(t):
            copy.wait_send()
    for phase in range(3):
        for copy in a2a_copies(phase):
            copy.wait_send()


def per_device(nl, nh, nw, positions, velocities, radius, counts, cell_index, fluid_velocity, plan):
    gl, gh, gw, slots = radius.shape
    bins = gl * gh * gw
    cap = max(2, 2 * bins // nl)
    spread = fluid_velocity.shape[1] // 128
    groups = nh * nw
    dims = (gl, gh, gw, cap, spread)

    def count(n):
        return 1 if n <= 2 else 2

    sl, sh, sw = count(nl), count(nh), count(nw)
    halos = sl * gh * gw + sh * gl * gw + sw * gl * gh
    blocks = gl * (gh * gw + 2 * (gh - 1) * gw + 2 * gh * (gw - 1)) + 2 * (gl - 1) * gh * gw + halos
    vmem = pltpu.VMEM
    scratch = [
        vmem(positions.shape, F32), vmem(velocities.shape, F32), vmem(radius.shape, F32), vmem((gh, gw, gl), jnp.int32),
        vmem(cell_index.shape, jnp.int32), vmem(fluid_velocity.shape, F32), vmem((1, bins), jnp.int32),
        pltpu.SemaphoreType.DMA((7,)),
        vmem((bins, 8, 128), F32), vmem((bins, 8, 128), F32), vmem((bins, 8, 128), F32),
        vmem((bins, 8, 128), F32), vmem((bins, 8, 128), F32),
        vmem((2, gl, gh, gw, 8, 128), F32),
        vmem((2, sl, gh, gw, 8, 128), F32), vmem((2, sh, gl, gw, 8, 128), F32), vmem((2, sw, gl, gh, 8, 128), F32),
        vmem((bins, 128, 32), BF16), vmem((bins, 32, 256), BF16), vmem((bins, 128, 384), F32),
        vmem((bins, 32, 128), F32), vmem((blocks, 128, 128), F32),
        vmem((gl, 128, gh * gw * 128), BF16),
        vmem((groups, 8, 128), F32), vmem((groups, 8, 128), F32), vmem((max(1, groups - 1), 8, 128), F32),
        vmem((nl, 2, cap, 128), F32), vmem((nl, 3, cap, 128), F32), vmem((nl, 3, cap, 128), F32),
        vmem((nl - 1, 2, cap, 128), F32), vmem((nl - 1, 3, cap, 128), F32), vmem((nl - 1, 3, cap, 128), F32),
        pltpu.SemaphoreType.DMA((2, 3, 2)), pltpu.SemaphoreType.DMA((2, 3, 2)),
        pltpu.SemaphoreType.DMA((2, groups)), pltpu.SemaphoreType.DMA((2, groups)),
        pltpu.SemaphoreType.DMA((3, nl)), pltpu.SemaphoreType.DMA((3, nl)),
    ]
    in_vmem = pl.BlockSpec(memory_space=pltpu.VMEM)
    anywhere = pl.BlockSpec(memory_space=pl.ANY)
    moved, fluid_next = pl.pallas_call(
        functools.partial(kernel, nl, nh, nw, dims),
        out_shape=(
            jax.ShapeDtypeStruct((8, nl * cap, slots), F32),
            jax.ShapeDtypeStruct(fluid_velocity.shape, F32),
        ),
        in_specs=[anywhere] * 7,
        out_specs=(in_vmem, in_vmem),
        scratch_shapes=scratch,
        compiler_params=pltpu.CompilerParams(
            collective_id=0, has_side_effects=True, vmem_limit_bytes=56 * 1024 * 1024
        ),
    )(positions, velocities, radius, counts.transpose(1, 2, 0), cell_index, fluid_velocity, plan.reshape(1, bins))
    return moved.reshape(8, 1, 1, nl * cap, slots), fluid_next


def solution(mesh):
    sizes = dict(mesh.shape)
    in_specs = (
        P(None, ("section", "len"), "ht", "wd", None),
        P(None, ("section", "len"), "ht", "wd", None),
        P(("section", "len"), "ht", "wd", None),
        P(("section", "len"), "ht", "wd"),
        P(("section", "len"), "ht", "wd", None),
        P(None, ("section", "len", "ht", "wd")),
        P(("section", "len"), "ht", "wd", None, None),
    )
    out_specs = (
        P(None, "ht", "wd", ("section", "len"), None),
        P(None, ("section", "len", "ht", "wd")),
    )
    body = functools.partial(per_device, sizes["len"], sizes["ht"], sizes["wd"])
    return jax.shard_map(body, mesh=mesh, in_specs=in_specs, out_specs=out_specs, check_vma=False)
```

```python
import functools

import jax
import jax.numpy as jnp
from jax import lax
from jax.experimental import pallas as pl
from jax.experimental.pallas import tpu as pltpu
from jax.sharding import PartitionSpec as P

STEP = 0.1
COUPLE = 0.5
RADIUS_REF = 0.45
PARK = 64.0
MESH = pl.DeviceIdType.MESH
F32 = jnp.float32
BF16 = jnp.bfloat16


def dot(a, b):
    return jnp.dot(a, b, preferred_element_type=F32)


def dot_t(a, b):
    return lax.dot_general(a, b, (((1,), (1,)), ((), ())), preferred_element_type=F32)


def split3(x):
    h = x.astype(BF16).astype(F32)
    rest = x - h
    m = rest.astype(BF16).astype(F32)
    return h, m, rest - m


def axis_sides(axis, n, size):
    me = lax.axis_index(axis)
    if n == 1:
        return []
    if n == 2:
        return [(1 - me, (size - 1) * (1 - me), size * (1 - me) - me, None)]
    return [(me - 1, 0, -1, me > 0), (me + 1, size - 1, size, me < n - 1)]


def maybe(cond, fn):
    if cond is None:
        fn()
    else:
        pl.when(cond)(fn)


def kernel(
    nl, nh, nw, dims,
    pos_hbm, vel_hbm, rad_hbm, cnt_hbm, cell_hbm, flu_hbm, plan_hbm,
    moved_ref, fnext_ref,
    pos_ref, vel_ref, rad_ref, cnt_ref, cell_ref, flu_ref, plan_ref, load_sem,
    xr, vr, ur, accr, lv, xp, hl, hh, hw, lt, rr, pc, gg, tc, oh, ft, pb, pr,
    out0, out1, out2, in0, in1, in2,
    halo_send, halo_recv, grp_send, grp_recv, a2a_send, a2a_recv,
):
    gl, gh, gw, cap, spread = dims
    bins = gl * gh * gw
    layer = gh * gw
    groups = nh * nw
    me_l = lax.axis_index("len")
    me_h = lax.axis_index("ht")
    me_w = lax.axis_index("wd")
    me_g = me_h * nw + me_w

    loads = []
    for k, (source, target) in enumerate((
        (pos_hbm, pos_ref), (vel_hbm, vel_ref), (rad_hbm, rad_ref), (cnt_hbm, cnt_ref),
        (cell_hbm, cell_ref), (flu_hbm, flu_ref), (plan_hbm, plan_ref),
    )):
        loads.append(pltpu.make_async_copy(source, target, load_sem.at[k]))
    for load in loads:
        load.start()

    barrier = pltpu.get_barrier_semaphore()

    def len_peer(k):
        return lax.rem(me_l + k, nl)

    def grp_peer(k):
        return lax.rem(me_g + k, groups)

    def grp_id(k):
        g = grp_peer(k)
        return {"ht": g // nw, "wd": lax.rem(g, nw)}

    for k in range(1, nl):
        pl.semaphore_signal(barrier, inc=1, device_id={"len": len_peer(k)}, device_id_type=MESH)
    for k in range(1, groups):
        pl.semaphore_signal(barrier, inc=1, device_id=grp_id(k), device_id_type=MESH)

    row = lax.broadcasted_iota(jnp.int32, (8, 128), 0)
    lane = lax.broadcasted_iota(jnp.int32, (1, 128), 1)
    layer_lane = lax.broadcasted_iota(jnp.int32, (1, gl), 1)

    for load in loads:
        load.wait()

    def load_layer(l, _):
        for h in range(gh):
            for w in range(gw):
                b = l * layer + h * gw + w
                xr[b] = jnp.zeros((8, 128), F32)
                vr[b] = jnp.zeros((8, 128), F32)
                for c in range(3):
                    xr[b, c : c + 1, :] = pos_ref[c, l, h, w : w + 1, :]
                    vr[b, c : c + 1, :] = vel_ref[c, l, h, w : w + 1, :]
                xr[b, 3:4, :] = rad_ref[l, h, w : w + 1, :]
                numbers = cnt_ref[h, w : w + 1, :].astype(F32)
                number = jnp.sum(jnp.where(layer_lane == l, numbers, 0.0), axis=1, keepdims=True)
                live = lane.astype(F32) < number
                lv[b] = jnp.broadcast_to(jnp.where(live, 1.0, 0.0), (8, 128))
                xp[0, l, h, w] = jnp.where((lv[b] > 0.5) | (row >= 3), xr[b], PARK)
        return 0

    lax.fori_loop(0, gl, load_layer, 0)
    for c in range(3):
        for s in range(spread):
            ft[0, c * spread + s : c * spread + s + 1, :] = flu_ref[c : c + 1, s * 128 : (s + 1) * 128]
    for r_ in range(3 * spread, 8):
        ft[0, r_ : r_ + 1, :] = jnp.zeros((1, 128), F32)

    plans = []
    for axis, n, size, ref in (("len", nl, gl, hl), ("ht", nh, gh, hh), ("wd", nw, gw, hw)):
        plans.append((axis, ref, axis_sides(axis, n, size)))
    empty = jnp.where(row < 3, PARK, RADIUS_REF)
    for axis, ref, sides in plans:
        for s, (partner, face, coord, exists) in enumerate(sides):
            if exists is not None:

                def fill(ref=ref, s=s):
                    for t in range(2):
                        ref[t, s] = jnp.broadcast_to(empty, ref.shape[2:])

                pl.when(jnp.logical_not(exists))(fill)

    pl.semaphore_wait(barrier, nl - 1 + groups - 1)

    def halo_copies(t):
        res = []
        for a, (axis, ref, sides) in enumerate(plans):
            for s, (partner, face, coord, exists) in enumerate(sides):
                back = s if len(sides) == 1 else 1 - s
                src = (xp.at[t, face], xp.at[t, :, face], xp.at[t, :, :, face])[a]
                send = pltpu.make_async_remote_copy(
                    src_ref=src, dst_ref=ref.at[t, back],
                    send_sem=halo_send.at[t, a, s], recv_sem=halo_recv.at[t, a, back],
                    device_id={axis: partner}, device_id_type=MESH,
                )
                recv = pltpu.make_async_remote_copy(
                    src_ref=src, dst_ref=ref.at[t, s],
                    send_sem=halo_send.at[t, a, s], recv_sem=halo_recv.at[t, a, s],
                    device_id={axis: partner}, device_id_type=MESH,
                )
                res.append((send, recv, exists))
        return res

    def start_halo(t):
        for send, recv, exists in halo_copies(t):
            maybe(exists, send.start)

    def wait_halo(t):
        for send, recv, exists in halo_copies(t):
            maybe(exists, recv.wait_recv)

    def wait_halo_sent(t):
        for send, recv, exists in halo_copies(t):
            maybe(exists, send.wait_send)

    def grp_copies(phase):
        res = []
        for k in range(1, groups):
            src = ft.at[0] if phase == 0 else pb.at[grp_peer(k)]
            dst = ft.at[k] if phase == 0 else pr.at[k - 1]
            res.append(pltpu.make_async_remote_copy(
                src_ref=src, dst_ref=dst, send_sem=grp_send.at[phase, k - 1],
                recv_sem=grp_recv.at[phase, k - 1], device_id=grp_id(k), device_id_type=MESH))
        return res

    def a2a_copies(phase):
        src, dst = ((out0, in0), (out1, in1), (out2, in2))[phase]
        res = []
        for k in range(1, nl):
            res.append(pltpu.make_async_remote_copy(
                src_ref=src.at[len_peer(k)], dst_ref=dst.at[k - 1], send_sem=a2a_send.at[phase, k - 1],
                recv_sem=a2a_recv.at[phase, k - 1], device_id={"len": len_peer(k)}, device_id_type=MESH))
        return res

    start_halo(0)
    for copy in grp_copies(0):
        copy.start()

    dest = plan_ref[...]
    marks = jnp.where(dest == lax.broadcasted_iota(jnp.int32, (16, bins), 0), 1.0, 0.0)
    before = jnp.where(
        lax.broadcasted_iota(jnp.int32, (bins, bins), 0) < lax.broadcasted_iota(jnp.int32, (bins, bins), 1),
        1.0, 0.0)
    earlier = dot(marks.astype(BF16), before.astype(BF16))
    rank = jnp.sum(earlier * marks, axis=0, keepdims=True)
    slot = dest * cap + rank.astype(jnp.int32)
    sel = jnp.where(slot == lax.broadcasted_iota(jnp.int32, (nl * cap, bins), 0), 1.0, 0.0)
    sel3 = jnp.concatenate([sel, sel, sel], axis=1).astype(BF16)

    def pack(values, out, c):
        parts = jnp.concatenate(split3(values), axis=0).astype(BF16)
        got = dot(sel3, parts)
        for d in range(nl):
            out[d, c] = got[d * cap : (d + 1) * cap]

    alive = lv[:, 0, :]
    pack(xr[:, 3, :] * alive, out0, 0)
    pack(alive, out0, 1)
    for copy in a2a_copies(0):
        copy.start()

    mid = ((gl - 1) / 2 + 0.5, gh / 2, gw / 2)

    def coords(tile, where):
        off = jnp.zeros((8, 128), F32)
        for c in range(3):
            off = jnp.where(row == c, jnp.asarray(where[c], F32) - mid[c], off)
        return jnp.where(row < 3, tile + off, 0.0)

    zero = jnp.zeros((8, 128), F32)
    part_row = lax.broadcasted_iota(jnp.int32, (32, 384), 0)
    part_comp = lax.broadcasted_iota(jnp.int32, (32, 384), 1) // 128
    spread_out = jnp.where((part_row == part_comp) | (part_row == part_comp + 16) | (part_row == part_comp + 27), 1.0, 0.0).astype(BF16)

    def rows_of(*values):
        out = zero
        for k, value in enumerate(values):
            if value is not None:
                out = jnp.where(row == k, value, out)
        return out

    def halves(place):
        return split3(place) + (split3(jnp.sum(place * place, axis=0, keepdims=True)),)

    def right_side(t, index, tile, place):
        h, m, l, (nh_, nm_, nl_) = halves(place)
        first = jnp.where(row < 3, 2.0 * h, rows_of(None, None, None, 1.0, nh_, None, None, 1.0))
        second = jnp.where(row < 3, 2.0 * m, jnp.where(row == 3, pltpu.roll(2.0 * l, 1, 0), rows_of(None, None, None, None, nm_)))
        third = jnp.where(row < 3, 2.0 * h, rows_of(None, None, None, 1.0, None, None, None, nl_))
        fourth = jnp.where(row < 3, 2.0 * m, jnp.where(row < 6, pltpu.roll(2.0 * h, 3, 0), pltpu.roll(2.0 * l, 6, 0)))
        rr[index, :, 0:128] = jnp.concatenate([first, second, third, fourth], axis=0).astype(BF16)
        if t == 0:
            rh, rm, _ = split3(tile[3:4])
            reach = [rows_of(None, None, None, None, None, 1.0, rh), rows_of(None, None, None, None, None, None, rm),
                     rows_of(None, None, None, None, None, 1.0), zero]
            rr[index, :, 128:256] = jnp.concatenate(reach, axis=0).astype(BF16)

    def left_side(tile, place):
        h, m, l, (nh_, nm_, nl_) = halves(place)
        rh, rm, _ = split3(tile[3:4])
        first = jnp.where(row < 3, h, rows_of(None, None, None, -nh_, -1.0, rh, 1.0, -nl_))
        third = jnp.where(row < 3, m, rows_of(None, None, None, -nm_, None, rm, None, -1.0))
        second = jnp.where(row == 3, pltpu.roll(h, 1, 0), first)
        fourth = jnp.where(row < 3, m, jnp.where(row < 6, pltpu.roll(l, 3, 0), pltpu.roll(h, 6, 0)))
        left = jnp.concatenate([first, second, third, fourth], axis=0).astype(BF16).T
        return left, dot(left, spread_out)

    def push(t, target, source, columns, block):
        if t == 0:
            both = dot(source, rr[target])
            dist = both[:, :128]
            inv = pl.reciprocal(both[:, 128:], approx=False)
            inv = inv * inv
            tc[block] = inv
        else:
            dist = dot(source, rr[target, :, 0:128])
            inv = tc[block]
        e = jnp.exp(dist * inv)
        acc = [None] * 4
        for k in range(16):
            piece = e[8 * k : 8 * k + 8]
            terms = [piece * columns[8 * k : 8 * k + 8, 128 * c : 128 * c + 128] for c in range(3)] + [piece]
            acc = terms if k == 0 else [a + b for a, b in zip(acc, terms)]
        return jnp.concatenate(acc, axis=0)

    near = []
    for h in range(gh):
        for w in range(gw):
            near.append((h * gw + w, h * gw + w))
            for h2, w2 in ((h - 1, w), (h + 1, w), (h, w - 1), (h, w + 1)):
                if 0 <= h2 < gh and 0 <= w2 < gw:
                    near.append((h * gw + w, h2 * gw + w2))
    per_layer = len(near)
    base_len = gl * per_layer
    base_halo = base_len + 2 * (gl - 1) * layer

    def prepare(t):
        def one(l, _):
            for h in range(gh):
                for w in range(gw):
                    b = l * layer + h * gw + w
                    tile = xp[t, l, h, w]
                    place = coords(tile, (l, h, w))
                    right_side(t, b, tile, place)
                    lt[b], pc[b] = left_side(tile, place)
            return 0

        lax.fori_loop(0, gl, one, 0)

    def interior(t):
        def one(l, _):
            base = l * layer
            sums = [None] * layer
            for n_, (i, j) in enumerate(near):
                got = push(t, base + i, lt[base + j], pc.at[base + j], l * per_layer + n_)
                sums[i] = got if sums[i] is None else sums[i] + got
            for n_ in range(layer):
                gg[base + n_] = sums[n_]
            return 0

        lax.fori_loop(0, gl, one, 0)

        def along(l, _):
            base = l * layer
            ups, downs = [], []
            for n_ in range(layer):
                block = base_len + 2 * (base + n_)
                ups.append(push(t, base + layer + n_, lt[base + n_], pc.at[base + n_], block))
                downs.append(push(t, base + n_, lt[base + layer + n_], pc.at[base + layer + n_], block + 1))
            for n_ in range(layer):
                gg[base + n_] += downs[n_]
                gg[base + layer + n_] += ups[n_]
            return 0

        lax.fori_loop(0, gl - 1, along, 0)

    def boundary(t):
        at = bins
        for s, (partner, face, coord, exists) in enumerate(plans[0][2]):
            sums = []
            for h in range(gh):
                for w in range(gw):
                    tile = hl[t, s, h, w]
                    source, columns = left_side(tile, coords(tile, (coord, h, w)))
                    n_ = h * gw + w
                    sums.append(push(t, face * layer + n_, source, columns, base_halo + at - bins + n_))
            for n_ in range(layer):
                gg[face * layer + n_] += sums[n_]
            at += layer
        for a, across in ((1, gw), (2, gh)):
            ref = plans[a][1]
            for s, (partner, face, coord, exists) in enumerate(plans[a][2]):
                step = 4 if gl % 4 == 0 else 1

                def one(p, _, ref=ref, s=s, face=face, coord=coord, a=a, across=across, at=at, step=step):
                    targets, sums = [], []
                    for q in range(step):
                        l = p * step + q
                        for y in range(across):
                            tile = ref[t, s, l, y]
                            place = coords(tile, (l, coord, y) if a == 1 else (l, y, coord))
                            source, columns = left_side(tile, place)
                            n_ = at + l * across + y
                            target = l * layer + (face * gw + y if a == 1 else y * gw + face)
                            targets.append(target)
                            sums.append(push(t, target, source, columns, base_halo + n_ - bins))
                    for target, got in zip(targets, sums):
                        gg[target] += got
                    return 0

                lax.fori_loop(0, gl // step, one, 0)
                at += gl * across

    lo_rows = lax.broadcasted_iota(jnp.int32, (128, 128), 0)

    def hi_mask(cells, g):
        return lax.shift_right_logical(cells, 7) == g * spread + lax.rem(row, spread)

    def read_fluid():
        for copy in grp_copies(0):
            copy.wait_recv()
        table = []
        for k in range(groups):
            table.append(ft[k])
        table = jnp.concatenate(table, axis=0)
        table = jnp.concatenate(split3(table), axis=0).astype(BF16)

        def one(l, _):
            for h in range(gh):
                for w in range(gw):
                    n_ = h * gw + w
                    cells = cell_ref[l, h, w : w + 1, :]
                    low = lax.rem(cells, 128)
                    oh[l, :, n_ * 128 : (n_ + 1) * 128] = jnp.where(low == lo_rows, 1.0, 0.0).astype(BF16)
            got = dot(table, oh[l])
            full = got[: groups * 8] + got[groups * 8 : groups * 16] + got[groups * 16 :]
            for h in range(gh):
                for w in range(gw):
                    n_ = h * gw + w
                    cells = cell_ref[l, h, w : w + 1, :]
                    mine = full[:, n_ * 128 : (n_ + 1) * 128]
                    u = jnp.zeros((8, 128), F32)
                    for k in range(groups):
                        g = lax.rem(me_g - k + groups, groups)
                        u = u + jnp.where(hi_mask(cells, g), mine[k * 8 : (k + 1) * 8], 0.0)
                    b = l * layer + n_
                    ur[b] = jnp.zeros((8, 128), F32)
                    for c in range(3):
                        ur[b, c : c + 1, :] = jnp.sum(u[c * spread : (c + 1) * spread], axis=0, keepdims=True)
            return 0

        lax.fori_loop(0, gl, one, 0)

    def update(t):
        def one(l, _):
            for h in range(gh):
                for w in range(gw):
                    b = l * layer + h * gw + w
                    tile = xr[b]
                    radius = tile[3:4]
                    ratio = radius * (1.0 / RADIUS_REF)
                    mass = ratio * ratio * ratio
                    place = coords(xp[t, l, h, w], (l, h, w))
                    g = gg[b]
                    rows = [jnp.sum(g[8 * c : 8 * c + 8], axis=0, keepdims=True) for c in range(4)]
                    total = jnp.concatenate(rows + rows, axis=0)
                    force = place * rows[3] - total
                    speed = vr[b]
                    drag = radius * (ur[b] - speed)
                    accr[b] = drag if t == 0 else accr[b] + drag
                    speed = speed + STEP * (force + drag) * (1.0 / mass)
                    alive = lv[b] > 0.5
                    speed = jnp.where((row < 3) & alive, speed, 0.0)
                    vr[b] = speed
                    if t == 0:
                        tile = tile + STEP * speed
                        xr[b] = tile
                        xp[1, l, h, w] = jnp.where(alive | (row >= 3), tile, PARK)
            return 0

        lax.fori_loop(0, gl, one, 0)

    prepare(0)
    interior(0)
    read_fluid()
    wait_halo(0)
    boundary(0)
    update(0)
    start_halo(1)
    for c in range(3):
        pack(xr[:, c, :] * alive, out1, c)
    for copy in a2a_copies(1):
        copy.start()

    prepare(1)
    interior(1)
    wait_halo(1)
    boundary(1)
    update(1)
    for c in range(3):
        pack(vr[:, c, :], out2, c)
    for copy in a2a_copies(2):
        copy.start()

    def cell_sums(l, total):
        lefts = []
        for h in range(gh):
            for w in range(gw):
                b = l * layer + h * gw + w
                cells = cell_ref[l, h, w : w + 1, :]
                radius = xr[b, 3:4, :]
                ratio = radius * (1.0 / RADIUS_REF)
                live_row = lv[b, 0:1, :]
                rows = [accr[b, c : c + 1, :] * live_row for c in range(3)] + [ratio * ratio * ratio * live_row]
                term = jnp.concatenate([rows[r_ // spread] for r_ in range(4 * spread)], axis=0)
                parts = split3(term)
                pieces = []
                for part in parts:
                    for g in range(groups):
                        pieces.append(jnp.where(hi_mask(cells, g), part, 0.0))
                lefts.append(jnp.concatenate(pieces, axis=0).astype(BF16))
        return total + dot_t(jnp.concatenate(lefts, axis=1), oh[l])

    sums = lax.fori_loop(0, gl, cell_sums, jnp.zeros((groups * 24, 128), F32))
    sums = sums[: groups * 8] + sums[groups * 8 : groups * 16] + sums[groups * 16 :]
    for g in range(groups):
        pb[g] = sums[g * 8 : (g + 1) * 8]
    for copy in grp_copies(1):
        copy.start()

    def landed(own, arrived, c, put):
        put(me_l, own[me_l, c])
        for k in range(1, nl):
            put(lax.rem(me_l - k + nl, nl), arrived[k - 1, c])

    for copy in a2a_copies(0) + a2a_copies(1):
        copy.wait_recv()
    for k in range(nl):
        source = lax.rem(me_l - k + nl, nl)
        at = pl.ds(source * cap, cap)
        early = out0.at[me_l] if k == 0 else in0.at[k - 1]
        for c in range(2):
            moved_ref[6 + c, at, :] = early[c]

    for copy in grp_copies(1):
        copy.wait_recv()
    whole = pb[me_g]
    for k in range(groups - 1):
        whole = whole + pr[k]
    mass_rows = whole[3 * spread : 4 * spread]
    for c in range(3):
        ratio = whole[c * spread : (c + 1) * spread] / (1.0 + mass_rows)
        fresh = ft[0, c * spread : (c + 1) * spread, :] - COUPLE * ratio
        for s in range(spread):
            fnext_ref[c : c + 1, s * 128 : (s + 1) * 128] = fresh[s : s + 1]

    for copy in a2a_copies(2):
        copy.wait_recv()
    for k in range(nl):
        source = lax.rem(me_l - k + nl, nl)
        at = pl.ds(source * cap, cap)
        place = out1.at[me_l] if k == 0 else in1.at[k - 1]
        speed = out2.at[me_l] if k == 0 else in2.at[k - 1]
        for c in range(3):
            v = speed[c]
            moved_ref[3 + c, at, :] = v
            moved_ref[c, at, :] = place[c] + STEP * v

    for t in range(2):
        wait_halo_sent(t)
        for copy in grp_copies(t):
            copy.wait_send()
    for phase in range(3):
        for copy in a2a_copies(phase):
            copy.wait_send()


def per_device(nl, nh, nw, positions, velocities, radius, counts, cell_index, fluid_velocity, plan):
    gl, gh, gw, slots = radius.shape
    bins = gl * gh * gw
    cap = max(2, 2 * bins // nl)
    spread = fluid_velocity.shape[1] // 128
    groups = nh * nw
    dims = (gl, gh, gw, cap, spread)

    def count(n):
        return 1 if n <= 2 else 2

    sl, sh, sw = count(nl), count(nh), count(nw)
    halos = sl * gh * gw + sh * gl * gw + sw * gl * gh
    blocks = gl * (gh * gw + 2 * (gh - 1) * gw + 2 * gh * (gw - 1)) + 2 * (gl - 1) * gh * gw + halos
    vmem = pltpu.VMEM
    scratch = [
        vmem(positions.shape, F32), vmem(velocities.shape, F32), vmem(radius.shape, F32), vmem((gh, gw, gl), jnp.int32),
        vmem(cell_index.shape, jnp.int32), vmem(fluid_velocity.shape, F32), vmem((1, bins), jnp.int32),
        pltpu.SemaphoreType.DMA((7,)),
        vmem((bins, 8, 128), F32), vmem((bins, 8, 128), F32), vmem((bins, 8, 128), F32),
        vmem((bins, 8, 128), F32), vmem((bins, 8, 128), F32),
        vmem((2, gl, gh, gw, 8, 128), F32),
        vmem((2, sl, gh, gw, 8, 128), F32), vmem((2, sh, gl, gw, 8, 128), F32), vmem((2, sw, gl, gh, 8, 128), F32),
        vmem((bins, 128, 32), BF16), vmem((bins, 32, 256), BF16), vmem((bins, 128, 384), F32),
        vmem((bins, 32, 128), F32), vmem((blocks, 128, 128), F32),
        vmem((gl, 128, gh * gw * 128), BF16),
        vmem((groups, 8, 128), F32), vmem((groups, 8, 128), F32), vmem((max(1, groups - 1), 8, 128), F32),
        vmem((nl, 2, cap, 128), F32), vmem((nl, 3, cap, 128), F32), vmem((nl, 3, cap, 128), F32),
        vmem((nl - 1, 2, cap, 128), F32), vmem((nl - 1, 3, cap, 128), F32), vmem((nl - 1, 3, cap, 128), F32),
        pltpu.SemaphoreType.DMA((2, 3, 2)), pltpu.SemaphoreType.DMA((2, 3, 2)),
        pltpu.SemaphoreType.DMA((2, groups)), pltpu.SemaphoreType.DMA((2, groups)),
        pltpu.SemaphoreType.DMA((3, nl)), pltpu.SemaphoreType.DMA((3, nl)),
    ]
    in_vmem = pl.BlockSpec(memory_space=pltpu.VMEM)
    anywhere = pl.BlockSpec(memory_space=pl.ANY)
    moved, fluid_next = pl.pallas_call(
        functools.partial(kernel, nl, nh, nw, dims),
        out_shape=(
            jax.ShapeDtypeStruct((8, nl * cap, slots), F32),
            jax.ShapeDtypeStruct(fluid_velocity.shape, F32),
        ),
        in_specs=[anywhere] * 7,
        out_specs=(in_vmem, in_vmem),
        scratch_shapes=scratch,
        compiler_params=pltpu.CompilerParams(
            collective_id=0, has_side_effects=True, vmem_limit_bytes=56 * 1024 * 1024
        ),
    )(positions, velocities, radius, counts.transpose(1, 2, 0), cell_index, fluid_velocity, plan.reshape(1, bins))
    return moved.reshape(8, 1, 1, nl * cap, slots), fluid_next


def solution(mesh):
    sizes = dict(mesh.shape)
    in_specs = (
        P(None, ("section", "len"), "ht", "wd", None),
        P(None, ("section", "len"), "ht", "wd", None),
        P(("section", "len"), "ht", "wd", None),
        P(("section", "len"), "ht", "wd"),
        P(("section", "len"), "ht", "wd", None),
        P(None, ("section", "len", "ht", "wd")),
        P(("section", "len"), "ht", "wd", None, None),
    )
    out_specs = (
        P(None, "ht", "wd", ("section", "len"), None),
        P(None, ("section", "len", "ht", "wd")),
    )
    body = functools.partial(per_device, sizes["len"], sizes["ht"], sizes["wd"])
    return jax.shard_map(body, mesh=mesh, in_specs=in_specs, out_specs=out_specs, check_vma=False)
```
